32 devices in a mesh: outer: 4 (over x, core), inner: 8 (over z, y).
Axes of the slice: x: 2, y: 2, z: 4, core: 2. Of those that a mesh axis runs over, the one named last changes fastest.
Arguments:
- queries: bfloat16 [4096, 4096], P(('outer', 'inner')), may hold values from -200 to 200
- keys: bfloat16 [4096, 1024], P(('outer', 'inner')), may hold values from -6 to 6
- values: bfloat16 [4096, 1024], P(('outer', 'inner')), may hold values from -6 to 6
- lengths: int32 [8], replicated, may hold values from 1 to 1024, as said below
- pack_order: int32 [8], replicated, may hold values from 0 to 7, as said below
Outputs:
- attended: bfloat16 [4096, 4096], P(('outer', 'inner'))
The draws below stay inside these ranges and needn't reach their ends.
Inputs may be any that keep to these rules, and one draw needn't show every extreme that they name: 8 lengths that sum to 4096; the document packed first, lengths[pack_order[0]], has exactly 1024 tokens. `pack_order`: each of 0 to 7 exactly once.
All inputs are finite; a program needn't handle non-finite values.
Results may differ from the reference program's by a relative error of at most 0.0046.
Values may be sent and summed in bfloat16 or wider, within the bound.
No kernel may reach another device: no remote copies, remote signals or barrier semaphores. Data moves between devices by JAX's collectives and lax.ppermute only.
A program may use at most 64 MiB of HBM per device.

```python
import jax
import jax.numpy as jnp
from jax import lax

HEADS = 32
KV_HEADS = 8
HD = 128
TOK_DEV = 128
HOPS = 8
MOST = 1024
TOKENS = 4096
NDOC = 8


def drawn_pair(key):
    keys_base = jnp.clip(jax.random.normal(jax.random.fold_in(key, 11), (TOKENS, KV_HEADS * HD), jnp.float32), -6.0, 6.0)
    queries_base = jnp.clip(jax.random.normal(jax.random.fold_in(key, 12), (TOKENS, HEADS * HD), jnp.float32), -6.0, 6.0)
    return (queries_base, keys_base)


def draw_queries(key, part):
    return drawn_pair(key)[0].astype(jnp.bfloat16)


def draw_keys(key, part):
    return drawn_pair(key)[1].astype(jnp.bfloat16)


def packed_documents(key):
    others = NDOC - 1
    remaining = TOKENS - MOST
    quotient = remaining // others
    leftover = remaining % others
    spread = max(min(quotient - 1, MOST - quotient - 1), 0)
    pairs = others // 2
    base = quotient + (jnp.arange(others, dtype=jnp.int32) < leftover).astype(jnp.int32)
    delta = jax.random.randint(jax.random.fold_in(key, 21), (pairs,), 0, spread + 1, dtype=jnp.int32)
    signed = jnp.concatenate([delta, -delta, jnp.zeros((others - 2 * pairs,), jnp.int32)])
    rest = jax.random.permutation(jax.random.fold_in(key, 22), (base + signed).astype(jnp.int32))
    in_order = jnp.concatenate([jnp.full((1,), MOST, jnp.int32), rest.astype(jnp.int32)])
    order = jax.random.permutation(jax.random.fold_in(key, 23), NDOC).astype(jnp.int32)
    lengths = jnp.zeros((NDOC,), jnp.int32).at[order].set(in_order)
    return (lengths, order)


def draw_lengths(key, part):
    return packed_documents(key)[0]


def draw_pack_order(key, part):
    return packed_documents(key)[1]


def levels(key, dims, cuts, smallest, high):
    gain, own = 1.0, jax.random.fold_in(key, 6)
    for position, parts in cuts:
        draws = jnp.exp(jax.random.uniform(jax.random.fold_in(own, position), (parts,), jnp.float32, smallest / len(cuts), high / len(cuts)))
        gain = gain * jnp.repeat(draws, dims[position] // parts).reshape([-1 if axis == position else 1 for axis in range(len(dims))])
    return gain


def gaussian(own_key, shape, scale, bound, pieces=(), kind=jnp.bfloat16):
    array = scale * jax.random.normal(own_key, shape, jnp.float32)
    if pieces:
        array = array * levels(own_key, shape, pieces, -0.22, 0.18)
    return jnp.clip(array, -bound, bound).astype(kind)


def setup_inputs(seed: int = 0) -> dict:
    streams_of = jax.random.split(jax.random.key(seed), 6)
    return {
        "queries": draw_queries(jax.random.fold_in(streams_of[5], 71), 0),
        "keys": draw_keys(jax.random.fold_in(streams_of[5], 71), 0),
        "values": gaussian(streams_of[2], (TOKENS, KV_HEADS * HD), 1.0, 6.0, ((0, 32),)),
        "lengths": draw_lengths(jax.random.fold_in(streams_of[5], 71), 0),
        "pack_order": draw_pack_order(jax.random.fold_in(streams_of[5], 71), 0),
    }


def segment_ids(lengths, pack_order, positions):
    placed = jnp.take(lengths, pack_order).astype(jnp.int32)
    doc_starts = (jnp.cumsum(placed) - placed).astype(jnp.int32)
    counted = (doc_starts[None, :] <= positions[:, None]).astype(jnp.int32)
    return lax.optimization_barrier(jnp.sum(counted, axis=1)).astype(jnp.int32) - 1

def reference(queries, keys, values, lengths, pack_order):
    shard_rows = TOK_DEV
    window = (HOPS + 1) * shard_rows
    group_size = HEADS // KV_HEADS
    padding = HOPS * shard_rows
    blocks_all = TOKENS // shard_rows
    key_pad = jnp.concatenate([jnp.zeros((padding, KV_HEADS * HD), keys.dtype), keys], axis=0)
    value_pad = jnp.concatenate([jnp.zeros((padding, KV_HEADS * HD), values.dtype), values], axis=0)

    def one_block(block_index):
        first_row = (block_index * shard_rows).astype(jnp.int32)
        query_rows = lax.dynamic_slice_in_dim(queries, first_row, shard_rows, 0)
        query_rows = query_rows.astype(jnp.float32).reshape(shard_rows, KV_HEADS, group_size, HD)
        key_rows = lax.dynamic_slice_in_dim(key_pad, first_row, window, 0)
        key_rows = key_rows.astype(jnp.float32).reshape(window, KV_HEADS, HD)
        value_rows = lax.dynamic_slice_in_dim(value_pad, first_row, window, 0)
        value_rows = value_rows.astype(jnp.float32).reshape(window, KV_HEADS, HD)
        query_pos = first_row + jnp.arange(shard_rows, dtype=jnp.int32)
        key_pos = first_row - padding + jnp.arange(window, dtype=jnp.int32)
        query_seg = segment_ids(lengths, pack_order, query_pos)
        key_seg = segment_ids(lengths, pack_order, key_pos)
        allowed = (key_pos[None, :] >= 0) & (key_pos[None, :] <= query_pos[:, None]) & (key_seg[None, :] == query_seg[:, None])
        scores = jnp.einsum('tgjd,kgd->gjtk', query_rows, key_rows) / jnp.sqrt(jnp.float32(HD))
        scores = jnp.where(allowed[None, None], scores, -jnp.inf)
        largest = lax.optimization_barrier(jnp.max(scores, axis=-1, keepdims=True))
        exps = jnp.exp(scores - largest)
        weights = (exps / lax.optimization_barrier(jnp.sum(exps, axis=-1, keepdims=True))).astype(jnp.bfloat16)
        weights = lax.optimization_barrier(weights).astype(jnp.float32)
        output = jnp.einsum('gjtk,kgd->tgjd', weights, value_rows)
        return output.reshape(shard_rows, HEADS * HD).astype(jnp.bfloat16)
    result = lax.map(one_block, jnp.arange(blocks_all, dtype=jnp.int32))
    return result.reshape(TOKENS, HEADS * HD)
```

```python
import functools
import math

import jax
import jax.numpy as jnp
from jax import lax
from jax.experimental import pallas as pl
from jax.experimental.pallas import tpu as pltpu
from jax.sharding import PartitionSpec as P

HD = 128
HOPS = 8
FIRST = 1024
AXES = ("outer", "inner")
NEG = -1e30
SCALE = math.log2(math.e) / math.sqrt(HD)
RING = (0, 2, 4, 6, 7, 5, 3, 1)
OWN, MATE, NONE = 0, 1, 2
VMEM_LIMIT = 40 * 1024 * 1024
UNROLL = 4
FLOPS = 2_000_000_000


def make_plan(groups, first_blocks):
    m = len(RING)
    n = groups * m
    place = {j: p for p, j in enumerate(RING)}

    def held(d, j):
        o, i = divmod(d, m)
        if j == i:
            return d
        if o % 2 == 0 or j < i:
            return o * m + j
        return ((o + 2) % groups) * m + j

    def uses(q, b):
        return 0 < q - b <= HOPS and not (b < first_blocks <= q)

    def user(d, b):
        return d if uses(d, b) else d ^ m if uses(d ^ m, b) else None

    ops = [("A", 1), ("B", 1), ("A", 2), ("B", 2), ("A", 3), ("B", 3), ("A", 4)]
    route = {}
    for op, s in ops:
        route[op, s] = {}
        for d in range(n):
            o, i = divmod(d, m)
            way = 1 if (o % 2 == 0) == (op == "A") else -1
            j = RING[(place[i] - way * s) % m]
            b = held(d, j)
            behind = RING[(place[i] - way) % m]
            (source,) = [e for e in range(behind, n, m) if (e // m) % 2 == o % 2 and held(e, j) == b]
            route[op, s][d] = (source, b)
    for op, s in reversed(ops):
        sends_on = {e for e, _ in route.get((op, s + 1), {}).values()}
        route[op, s] = {d: r for d, r in route[op, s].items() if user(d, r[1]) is not None or d in sends_on}
    route["A", 4] = {user(d, b): (e, b) for d, (e, b) in route["A", 4].items()}
    return route, user


def block_table(route, user, groups):
    m = len(RING)
    n = groups * m
    rows = []
    for d in range(n):
        row = []
        for key in [("A", 1), ("B", 1), ("A", 2), ("B", 2), ("A", 3), ("B", 3), ("A", 4)]:
            if d not in route[key]:
                row += [0, NONE]
                continue
            b = route[key][d][1]
            u = d if key == ("A", 4) else user(d, b)
            row += [b, NONE if u is None else OWN if u == d else MATE]
        o = d // m
        row += [0, NONE] if o < 2 else [d if o % 2 == 0 else d - 2 * m, MATE]
        rows.append(row)
    return rows


def position(axes):
    outer, inner = axes
    return lax.axis_index(outer) * lax.axis_size(inner) + lax.axis_index(inner)


def doc_starts(lengths_ref, order_ref, fold, initial):
    def step(j, carry):
        start, value = carry
        value = fold(value, start)
        return start + lengths_ref[order_ref[j]], value

    return lax.fori_loop(0, order_ref.shape[0], step, (jnp.int32(0), initial), unroll=order_ref.shape[0] <= 8)[1]


def mask_bias(lengths_ref, order_ref, query_base, key_base, rows):
    query_pos = query_base + lax.broadcasted_iota(jnp.int32, (8, rows), 1)
    seen = doc_starts(
        lengths_ref,
        order_ref,
        lambda first, start: jnp.where(start <= query_pos, start, first),
        jnp.zeros((8, rows), jnp.int32),
    )
    seen, query_pos = (jnp.concatenate([x] * (rows // 8), axis=0) for x in (seen, query_pos))
    key_pos = key_base + lax.broadcasted_iota(jnp.int32, (rows, rows), 0)
    return jnp.where((key_pos >= seen) & (key_pos <= query_pos), 0.0, NEG).astype(jnp.float32)


def first_seen(lengths_ref, order_ref, query_base):
    return doc_starts(
        lengths_ref, order_ref, lambda first, start: jnp.where(start <= query_base, start, first), jnp.int32(0)
    )


def part_of(ref, g, width):
    return ref[:, pl.ds(pl.multiple_of(g * width, width), width)]


def attend_block(sizes, qt_of, kv_ref, bias, state, u, fresh):
    kv_heads, group_size, _ = sizes
    acc_ref, max_ref, sum_ref = state
    bias = jnp.concatenate([bias] * group_size, axis=1)

    def per_head(g, _):
        s = jnp.dot(part_of(kv_ref, g, HD), qt_of(g), preferred_element_type=jnp.float32)
        s = s * SCALE + bias
        top = jnp.max(s, axis=0, keepdims=True)
        if not fresh:
            old = max_ref[u, g]
            top = jnp.maximum(old, top)
            fade = jnp.exp2(old - top)
        p = jnp.exp2(s - top)
        total = jnp.sum(p, axis=0, keepdims=True)
        mixed = jnp.dot(part_of(kv_ref, kv_heads + g, HD), p.astype(jnp.bfloat16), preferred_element_type=jnp.float32)
        max_ref[u, g] = top
        sum_ref[u, g] = total if fresh else sum_ref[u, g] * fade + total
        acc_ref[u, g] = mixed if fresh else acc_ref[u, g] * fade + mixed
        return _

    lax.fori_loop(0, kv_heads, per_head, 0, unroll=UNROLL)


def pack_kv_kernel(k_ref, v_ref, kv_ref):
    width = k_ref.shape[1]
    kv_ref[:, :width] = k_ref[...]
    for g in range(width // HD):
        kv_ref[:, width + g * HD : width + (g + 1) * HD] = v_ref[:, g * HD : (g + 1) * HD].T


def own_kernel(sizes, mated, lengths_ref, order_ref, *refs):
    kv_heads, group_size, rows = sizes
    q_ref, kv_ref, qt_ref, *state = refs[1:] if mated else refs
    for h in range(kv_heads * group_size):
        qt_ref[:, h * HD : (h + 1) * HD] = q_ref[:, h * HD : (h + 1) * HD].T
    base = position(AXES) * rows
    bias = mask_bias(lengths_ref, order_ref, base, base, rows)
    attend_block(sizes, lambda g: part_of(qt_ref, g, group_size * HD), kv_ref, bias, state, OWN, True)


def block_of(table_ref, slot):
    device = position(AXES)
    if table_ref is None:
        block = device - 1 - slot
        return device, device, jnp.maximum(block, 0), jnp.where(block < 0, NONE, OWN)
    return device, table_ref[device, 0], table_ref[device, 1 + 2 * slot], table_ref[device, 2 + 2 * slot]


def back_kernel(sizes, slot, lengths_ref, order_ref, table_ref, qm_ref, kv_ref, *refs):
    kv_heads, group_size, rows = sizes
    state = refs[3:]
    _, mate, block, use = block_of(table_ref, slot)
    query_base, key_base = mate * rows, block * rows
    live = (use == MATE) & (key_base + rows > first_seen(lengths_ref, order_ref, query_base))

    @pl.when(live)
    def _():
        bias = mask_bias(lengths_ref, order_ref, query_base, key_base, rows)
        attend_block(sizes, lambda g: part_of(qm_ref, g, group_size * HD), kv_ref, bias, state, MATE, True)

    @pl.when(jnp.logical_not(live))
    def _():
        for g in range(kv_heads):
            for ref, value in zip(state, (0.0, NEG, 0.0)):
                ref[MATE, g] = jnp.full(ref.shape[2:], value, jnp.float32)


def add_block(sizes, slot, table_ref, lengths_ref, order_ref, q_ref, qm_ref, kv_ref, state):
    kv_heads, group_size, rows = sizes
    device, mate, block, use = block_of(table_ref, slot)
    mine = use == OWN
    query_base = jnp.where(mine, device, mate) * rows
    key_base = block * rows
    live = (use != NONE) & (key_base + rows > first_seen(lengths_ref, order_ref, query_base))

    @pl.when(live)
    def _():
        bias = mask_bias(lengths_ref, order_ref, query_base, key_base, rows)

        def qt_of(g):
            a = part_of(q_ref, g, group_size * HD)
            return a if qm_ref is None else jnp.where(mine, a, part_of(qm_ref, g, group_size * HD))

        attend_block(sizes, qt_of, kv_ref, bias, state, use, False)


def add_kernel(sizes, slot, mated, lengths_ref, order_ref, *refs):
    table_ref, refs = (refs[0], refs[1:]) if mated else (None, refs)
    q_ref, refs = refs[0], refs[1:]
    qm_ref, refs = (refs[0], refs[1:]) if mated else (None, refs)
    add_block(sizes, slot, table_ref, lengths_ref, order_ref, q_ref, qm_ref, refs[0], refs[4:])


def split3(x):
    a = x.astype(jnp.bfloat16)
    rest = x - a.astype(jnp.float32)
    b = rest.astype(jnp.bfloat16)
    return a, b, (rest - b.astype(jnp.float32)).astype(jnp.bfloat16)


def part_kernel(sizes, slot, lengths_ref, order_ref, table_ref, q_ref, qm_ref, kv_ref, a_in, m_in, s_in, part_ref, *state):
    kv_heads, group_size, rows = sizes
    add_block(sizes, slot, table_ref, lengths_ref, order_ref, q_ref, qm_ref, kv_ref, state)
    acc_ref, max_ref, sum_ref = state
    width = group_size * HD
    heads = kv_heads * group_size
    tops, sums = [], []
    for g in range(kv_heads):
        top, total = max_ref[MATE, g], sum_ref[MATE, g]
        share = 1.0 / jnp.where(total > 0, total, 1.0)
        part_ref[:, g * width : (g + 1) * width] = (acc_ref[MATE, g] * share).astype(jnp.bfloat16)
        for j in range(group_size):
            tops.append(top[:, j * HD : (j + 1) * HD])
            sums.append(total[:, j * HD : (j + 1) * HD])
    for column, stats in enumerate((tops, sums)):
        place = (heads + column) * HD
        for k, piece in enumerate(split3(jnp.concatenate(stats, axis=0))):
            part_ref[k * heads : (k + 1) * heads, place : place + HD] = piece


def last_kernel(sizes, slot, mated, lengths_ref, order_ref, *refs):
    table_ref, refs = (refs[0], refs[1:]) if mated else (None, refs)
    q_ref, refs = refs[0], refs[1:]
    kv_heads, group_size, rows = sizes
    heads = kv_heads * group_size
    part_ref, refs = (refs[0], refs[1:]) if mated else (None, refs)
    out_ref, state = refs[4], refs[5:]
    add_block(sizes, slot, table_ref, lengths_ref, order_ref, q_ref, None, refs[0], state)
    acc_ref, max_ref, sum_ref = state
    width = group_size * HD
    if mated:
        tops, sums = (
            sum(part_ref[k * heads : (k + 1) * heads, c * HD : (c + 1) * HD].astype(jnp.float32) for k in range(3))
            for c in (heads, heads + 1)
        )
        device = position(AXES)
        met = table_ref[device, 0] != device
        tops, sums = jnp.where(met, tops, NEG), jnp.where(met, sums, 0.0)
    for g in range(kv_heads):
        for j in range(group_size):
            h, mine = g * group_size + j, slice(j * HD, (j + 1) * HD)
            numer, top, total = acc_ref[OWN, g, :, mine], max_ref[OWN, g, :, mine], sum_ref[OWN, g, :, mine]
            if mated:
                both = jnp.maximum(top, tops[h : h + 1])
                weight, other = jnp.exp2(top - both), jnp.exp2(tops[h : h + 1] - both) * sums[h : h + 1]
                share = 1.0 / (total * weight + other)
                theirs = jnp.where(met, part_ref[:, h * HD : (h + 1) * HD].astype(jnp.float32), 0.0)
                out = numer * (weight * share) + theirs * (other * share)
            else:
                out = numer * (1.0 / total)
            out_ref[:, h * HD : (h + 1) * HD] = out.astype(jnp.bfloat16).T


def calls(sizes, scalars, mated):
    kv_heads, group_size, rows = sizes
    tall = group_size * rows
    sets = 2 if mated else 1
    state = [
        pltpu.VMEM((sets, kv_heads, HD, tall), jnp.float32),
        pltpu.VMEM((sets, kv_heads, 1, tall), jnp.float32),
        pltpu.VMEM((sets, kv_heads, 1, tall), jnp.float32),
    ]
    smem, vmem = pl.BlockSpec(memory_space=pltpu.SMEM), pl.BlockSpec(memory_space=pltpu.VMEM)
    held = []

    def call(kernel, arrays, out, name, keeps=True):
        n_in = len(scalars) + len(arrays)
        out = out + (state if keeps else [])
        result = pl.pallas_call(
            kernel,
            out_shape=out,
            in_specs=[smem] * len(scalars) + [vmem] * (len(arrays) + len(held)),
            out_specs=[vmem] * len(out),
            input_output_aliases={n_in + k: len(out) - 3 + k for k in range(len(held))},
            compiler_params=pltpu.CompilerParams(vmem_limit_bytes=VMEM_LIMIT),
            cost_estimate=pl.CostEstimate(flops=FLOPS, bytes_accessed=1 << 20, transcendentals=0),
            name=name,
        )(*scalars, *arrays, *held)
        held[:] = result[-3:]
        return result[:-3]

    def own(q, kv):
        qt = jax.ShapeDtypeStruct(q.shape, q.dtype)
        return call(functools.partial(own_kernel, sizes, mated), [q, kv], [qt], "own_block")[0]

    def back(slot, qm, kv):
        call(functools.partial(back_kernel, sizes, slot), [qm, kv], [], "mate_first_block")

    def add(slot, q, qm, kv):
        qs = [q] if qm is None else [q, qm]
        call(functools.partial(add_kernel, sizes, slot, qm is not None), qs + [kv], [], "add_block")

    def part(slot, q, qm, kv):
        out = jax.ShapeDtypeStruct((rows, (kv_heads * group_size + 2) * HD), jnp.bfloat16)
        return call(functools.partial(part_kernel, sizes, slot), [q, qm, kv], [out], "mate_part")[0]

    def last(slot, q, parts, kv):
        out = jax.ShapeDtypeStruct((rows, kv_heads * group_size * HD), jnp.bfloat16)
        return call(functools.partial(last_kernel, sizes, slot, mated), [q, *parts, kv], [out], "last_block")[0]

    return own, back, add, part, last


def pack_kv(keys, values):
    rows, width = keys.shape
    return pl.pallas_call(
        pack_kv_kernel, out_shape=jax.ShapeDtypeStruct((rows, 2 * width), keys.dtype), name="pack_keys_values"
    )(keys, values)


def ring_shards(groups, queries, keys, values, lengths, pack_order):
    rows, kv_heads = queries.shape[0], keys.shape[1] // HD
    m = len(RING)
    sizes = (kv_heads, queries.shape[1] // keys.shape[1], rows)
    route, user = make_plan(groups, FIRST // rows)
    mate_of = [d if d < 2 * m else d ^ m for d in range(groups * m)]
    table = jnp.array([[mate] + row for mate, row in zip(mate_of, block_table(route, user, groups))], jnp.int32)
    own, back, add, part, last = calls(sizes, (lengths, pack_order, table), True)

    def send(block, op, step):
        return lax.ppermute(block, AXES, sorted((e, d) for d, (e, _) in route[op, step].items()))

    mates = [(d, d ^ m) for d in range(2 * m, groups * m)]
    eight_back = [(m + i, 3 * m + i) for i in range(m)] + [(2 * m + i, 2 * m + i) for i in range(m)]
    kv = pack_kv(keys, values)
    a1 = send(kv, "A", 1)
    q = own(queries, kv)
    b1 = send(kv, "B", 1)
    qm = lax.ppermute(q, AXES, mates)
    kv8 = lax.ppermute(kv, AXES, eight_back)
    a2 = send(a1, "A", 2)
    back(7, qm, kv8)
    add(0, q, qm, a1)
    b2 = send(b1, "B", 2)
    add(1, q, qm, b1)
    a3 = send(a2, "A", 3)
    add(2, q, qm, a2)
    b3 = send(b2, "B", 3)
    add(3, q, qm, b2)
    a4 = send(a3, "A", 4)
    add(4, q, qm, a3)
    mine = part(5, q, qm, b3)
    theirs = lax.ppermute(mine, AXES, mates)
    return last(6, q, [theirs], a4)


def chain_shards(queries, keys, values, lengths, pack_order):
    rows, kv_heads = queries.shape[0], keys.shape[1] // HD
    sizes = (kv_heads, queries.shape[1] // keys.shape[1], rows)
    n = lax.axis_size(AXES)
    own, back, add, part, last = calls(sizes, (lengths, pack_order), False)
    kv = pack_kv(keys, values)
    q = own(queries, kv)
    for hop in range(HOPS):
        kv = lax.ppermute(kv, AXES, [(d, d + 1) for d in range(n - 1)])
        if hop < HOPS - 1:
            add(hop, q, None, kv)
    return last(HOPS - 1, q, [], kv)


def solution(mesh):
    spec, whole = P(AXES, None), P()
    outer, inner = mesh.shape["outer"], mesh.shape["inner"]
    ring = outer == 4 and inner == len(RING) == HOPS
    shards = functools.partial(ring_shards, outer) if ring else chain_shards
    return jax.shard_map(
        shards, mesh=mesh, in_specs=(spec, spec, spec, whole, whole), out_specs=spec, check_vma=False
    )
```

```python
import functools
import math

import jax
import jax.numpy as jnp
from jax import lax
from jax.experimental import pallas as pl
from jax.experimental.pallas import tpu as pltpu
from jax.sharding import PartitionSpec as P

HD = 128
HOPS = 8
FIRST = 1024
AXES = ("outer", "inner")
NEG = -1e30
SCALE = math.log2(math.e) / math.sqrt(HD)
RING = (0, 2, 4, 6, 7, 5, 3, 1)
OWN, MATE, NONE = 0, 1, 2
VMEM_LIMIT = 40 * 1024 * 1024
SLOTS = 8
STARTS = 2 + 2 * SLOTS
INFO_SPACE = pltpu.SMEM
FLOPS = 800_000_000
LAST_FLOPS = 50_000_000_000


def make_plan(groups, first_blocks):
    m = len(RING)
    n = groups * m
    place = {j: p for p, j in enumerate(RING)}

    def held(d, j):
        o, i = divmod(d, m)
        if j == i:
            return d
        if o % 2 == 0 or j < i:
            return o * m + j
        return ((o + 2) % groups) * m + j

    def uses(q, b):
        return 0 < q - b <= HOPS and not (b < first_blocks <= q)

    def user(d, b):
        return d if uses(d, b) else d ^ m if uses(d ^ m, b) else None

    ops = [("A", 1), ("B", 1), ("A", 2), ("B", 2), ("A", 3), ("B", 3), ("A", 4)]
    route = {}
    for op, s in ops:
        route[op, s] = {}
        for d in range(n):
            o, i = divmod(d, m)
            way = 1 if (o % 2 == 0) == (op == "A") else -1
            j = RING[(place[i] - way * s) % m]
            b = held(d, j)
            behind = RING[(place[i] - way) % m]
            (source,) = [e for e in range(behind, n, m) if (e // m) % 2 == o % 2 and held(e, j) == b]
            route[op, s][d] = (source, b)
    for op, s in reversed(ops):
        sends_on = {e for e, _ in route.get((op, s + 1), {}).values()}
        route[op, s] = {d: r for d, r in route[op, s].items() if user(d, r[1]) is not None or d in sends_on}
    route["A", 4] = {user(d, b): (e, b) for d, (e, b) in route["A", 4].items()}
    return route, user


def block_table(route, user, groups):
    m = len(RING)
    n = groups * m
    rows = []
    for d in range(n):
        row = []
        for key in [("A", 1), ("B", 1), ("A", 2), ("B", 2), ("A", 3), ("B", 3), ("A", 4)]:
            if d not in route[key]:
                row += [0, NONE]
                continue
            b = route[key][d][1]
            u = d if key == ("A", 4) else user(d, b)
            row += [b, NONE if u is None else OWN if u == d else MATE]
        o = d // m
        row += [0, NONE] if o < 2 else [d if o % 2 == 0 else d - 2 * m, MATE]
        rows.append(row)
    return rows


def position(axes):
    outer, inner = axes
    return lax.axis_index(outer) * lax.axis_size(inner) + lax.axis_index(inner)


def attend_block(sizes, q_of, kv_ref, bias, state, u, fresh):
    kv_heads, group_size, _ = sizes
    acc_ref, max_ref, sum_ref = state
    tile = 2 if group_size % 2 == 0 else 1
    bias = jnp.concatenate([bias] * tile, axis=1)
    for g in range(kv_heads):
        keys = kv_ref[:, g * HD : (g + 1) * HD]
        values = kv_ref[:, (kv_heads + g) * HD : (kv_heads + g + 1) * HD]
        for j in range(0, group_size, tile):
            columns = slice(j * HD, (j + tile) * HD)
            queries = jnp.concatenate([q_of(g * group_size + j + k) for k in range(tile)], axis=0)
            s = lax.dot_general(keys, queries, (((1,), (1,)), ((), ())), preferred_element_type=jnp.float32)
            s = s * SCALE + bias
            top = jnp.max(s, axis=0, keepdims=True)
            if not fresh:
                old = max_ref[u, g, :, columns]
                top = jnp.maximum(old, top)
                fade = jnp.exp2(old - top)
            p = jnp.exp2(s - top)
            total = jnp.sum(p, axis=0, keepdims=True)
            mixed = jnp.dot(values, p.astype(jnp.bfloat16), preferred_element_type=jnp.float32)
            max_ref[u, g, :, columns] = top
            sum_ref[u, g, :, columns] = total if fresh else sum_ref[u, g, :, columns] * fade + total
            acc_ref[u, g, :, columns] = mixed if fresh else acc_ref[u, g, :, columns] * fade + mixed


def head_of(ref):
    return lambda h: ref[:, h * HD : (h + 1) * HD]


def mask_bias(info_ref, n_docs, query_base, key_base, rows):
    query_pos = query_base + lax.broadcasted_iota(jnp.int32, (8, rows), 1)

    def latest(j, seen):
        start = info_ref[STARTS + j]
        return jnp.where(start <= query_pos, start, seen)

    seen = lax.fori_loop(0, n_docs, latest, jnp.zeros((8, rows), jnp.int32), unroll=n_docs <= 8)
    seen, query_pos = (jnp.concatenate([x] * (rows // 8), axis=0) for x in (seen, query_pos))
    key_pos = key_base + lax.broadcasted_iota(jnp.int32, (rows, rows), 0)
    return jnp.where((key_pos >= seen) & (key_pos <= query_pos), 0.0, NEG).astype(jnp.float32)


def pack_kernel(rows, n_docs, table, *refs):
    *far, k_ref, v_ref, kv_ref, info_ref, v_here, lengths_ref, order_ref, row_ref, sems = refs
    width = k_ref.shape[1]
    device = position(AXES)
    fetch_v = pltpu.make_async_copy(v_ref, v_here, sems.at[0])
    fetch_k = pltpu.make_async_copy(k_ref, kv_ref.at[:, pl.ds(0, width)], sems.at[1])
    small = [(far[0], lengths_ref), (far[1], order_ref)] + ([(far[2].at[device], row_ref)] if table else [])
    fetches = [pltpu.make_async_copy(a, b, sems.at[2 + k]) for k, (a, b) in enumerate(small)]
    for fetch in [fetch_v, fetch_k, *fetches]:
        fetch.start()
    for fetch in fetches:
        fetch.wait()

    mate = row_ref[0] if table else device
    info_ref[0] = device
    info_ref[1] = mate
    own_first, mate_first = device * rows, mate * rows

    def document(j, carry):
        start, own_seen, mate_seen = carry
        info_ref[STARTS + j] = start
        own_seen = jnp.where(start <= own_first, start, own_seen)
        mate_seen = jnp.where(start <= mate_first, start, mate_seen)
        return start + lengths_ref[order_ref[j]], own_seen, mate_seen

    zero = jnp.int32(0)
    _, own_seen, mate_seen = lax.fori_loop(0, n_docs, document, (zero, zero, zero), unroll=n_docs <= 8)
    for slot in range(SLOTS):
        if table:
            block, use = row_ref[1 + 2 * slot], row_ref[2 + 2 * slot]
        else:
            block, use = device - 1 - slot, OWN
        seen = jnp.where(use == OWN, own_seen, mate_seen)
        shown = (block >= 0) & (block * rows + rows > seen)
        info_ref[2 + 2 * slot] = block
        info_ref[3 + 2 * slot] = jnp.where(shown, use, NONE)

    fetch_v.wait()
    for g in range(width // HD):
        kv_ref[:, width + g * HD : width + (g + 1) * HD] = v_here[:, g * HD : (g + 1) * HD].T
    fetch_k.wait()


def own_kernel(sizes, n_docs, info_ref, q_ref, kv_ref, *state):
    rows = sizes[2]
    base = info_ref[0] * rows
    bias = mask_bias(info_ref, n_docs, base, base, rows)
    attend_block(sizes, head_of(q_ref), kv_ref, bias, state, OWN, True)


def back_kernel(sizes, n_docs, slot, info_ref, qm_ref, kv_ref, *refs):
    kv_heads, group_size, rows = sizes
    state = refs[3:]
    live = info_ref[3 + 2 * slot] == MATE

    @pl.when(live)
    def _():
        bias = mask_bias(info_ref, n_docs, info_ref[1] * rows, info_ref[2 + 2 * slot] * rows, rows)
        attend_block(sizes, head_of(qm_ref), kv_ref, bias, state, MATE, True)

    @pl.when(jnp.logical_not(live))
    def _():
        for g in range(kv_heads):
            for ref, value in zip(state, (0.0, NEG, 0.0)):
                ref[MATE, g] = jnp.full(ref.shape[2:], value, jnp.float32)


def add_block(sizes, n_docs, slot, info_ref, q_ref, qm_ref, kv_ref, state):
    rows = sizes[2]
    use = info_ref[3 + 2 * slot]

    @pl.when(use != NONE)
    def _():
        mine = use == OWN
        query_base = jnp.where(mine, info_ref[0], info_ref[1]) * rows
        bias = mask_bias(info_ref, n_docs, query_base, info_ref[2 + 2 * slot] * rows, rows)
        q_of = head_of(q_ref)
        if qm_ref is not None:
            q_own, q_mate = q_of, head_of(qm_ref)
            q_of = lambda h: jnp.where(mine, q_own(h), q_mate(h))
        attend_block(sizes, q_of, kv_ref, bias, state, use, False)


def add_kernel(sizes, n_docs, slot, mated, info_ref, q_ref, *refs):
    qm_ref, refs = (refs[0], refs[1:]) if mated else (None, refs)
    add_block(sizes, n_docs, slot, info_ref, q_ref, qm_ref, refs[0], refs[4:])


def split3(x):
    a = x.astype(jnp.bfloat16)
    rest = x - a.astype(jnp.float32)
    b = rest.astype(jnp.bfloat16)
    return a, b, (rest - b.astype(jnp.float32)).astype(jnp.bfloat16)


def part_kernel(sizes, n_docs, slot, info_ref, q_ref, qm_ref, kv_ref, a_in, m_in, s_in, part_ref, *state):
    kv_heads, group_size, rows = sizes
    add_block(sizes, n_docs, slot, info_ref, q_ref, qm_ref, kv_ref, state)
    acc_ref, max_ref, sum_ref = state
    width = group_size * HD
    heads = kv_heads * group_size
    tops, sums = [], []
    for g in range(kv_heads):
        top, total = max_ref[MATE, g], sum_ref[MATE, g]
        share = 1.0 / jnp.where(total > 0, total, 1.0)
        part_ref[:, g * width : (g + 1) * width] = (acc_ref[MATE, g] * share).astype(jnp.bfloat16)
        for j in range(group_size):
            tops.append(top[:, j * HD : (j + 1) * HD])
            sums.append(total[:, j * HD : (j + 1) * HD])
    for column, stats in enumerate((tops, sums)):
        place = (heads + column) * HD
        for k, piece in enumerate(split3(jnp.concatenate(stats, axis=0))):
            part_ref[k * heads : (k + 1) * heads, place : place + HD] = piece


def merge_kernel(sizes, mated, info_ref, *refs):
    kv_heads, group_size, rows = sizes
    heads = kv_heads * group_size
    part_ref, refs = (refs[0], refs[1:]) if mated else (None, refs)
    acc_ref, max_ref, sum_ref, out_ref = refs
    if mated:
        tops, sums = (
            sum(part_ref[k * heads : (k + 1) * heads, c * HD : (c + 1) * HD].astype(jnp.float32) for k in range(3))
            for c in (heads, heads + 1)
        )
        met = info_ref[1] != info_ref[0]
        tops, sums = jnp.where(met, tops, NEG), jnp.where(met, sums, 0.0)
    for g in range(kv_heads):
        for j in range(group_size):
            h, mine = g * group_size + j, slice(j * HD, (j + 1) * HD)
            numer, top, total = acc_ref[OWN, g, :, mine], max_ref[OWN, g, :, mine], sum_ref[OWN, g, :, mine]
            if mated:
                both = jnp.maximum(top, tops[h : h + 1])
                weight, other = jnp.exp2(top - both), jnp.exp2(tops[h : h + 1] - both) * sums[h : h + 1]
                share = 1.0 / (total * weight + other)
                theirs = jnp.where(met, part_ref[:, h * HD : (h + 1) * HD].astype(jnp.float32), 0.0)
                out = numer * (weight * share) + theirs * (other * share)
            else:
                out = numer * (1.0 / total)
            out_ref[:, h * HD : (h + 1) * HD] = out.astype(jnp.bfloat16).T


def calls(sizes, n_docs, info, mated):
    kv_heads, group_size, rows = sizes
    tall = group_size * rows
    sets = 2 if mated else 1
    state = [
        pltpu.VMEM((sets, kv_heads, HD, tall), jnp.float32),
        pltpu.VMEM((sets, kv_heads, 1, tall), jnp.float32),
        pltpu.VMEM((sets, kv_heads, 1, tall), jnp.float32),
    ]
    smem, vmem = pl.BlockSpec(memory_space=pltpu.SMEM), pl.BlockSpec(memory_space=pltpu.VMEM)
    held = []

    def call(kernel, arrays, out, name, keeps=True, flops=FLOPS):
        n_in = 1 + len(arrays)
        out = out + (state if keeps else [])
        result = pl.pallas_call(
            kernel,
            out_shape=out,
            in_specs=[smem] + [vmem] * (len(arrays) + len(held)),
            out_specs=[vmem] * len(out),
            input_output_aliases={n_in + k: len(out) - 3 + k for k in range(len(held))} if keeps else {},
            compiler_params=pltpu.CompilerParams(vmem_limit_bytes=VMEM_LIMIT),
            cost_estimate=pl.CostEstimate(flops=flops, bytes_accessed=1 << 20, transcendentals=0),
            name=name,
        )(info, *arrays, *held)
        if not keeps:
            return result
        held[:] = result[-3:]
        return result[:-3]

    def own(q, kv):
        call(functools.partial(own_kernel, sizes, n_docs), [q, kv], [], "own_block")

    def back(slot, qm, kv):
        call(functools.partial(back_kernel, sizes, n_docs, slot), [qm, kv], [], "mate_first_block")

    def add(slot, q, qm, kv, flops=FLOPS):
        qs = [q] if qm is None else [q, qm]
        kernel = functools.partial(add_kernel, sizes, n_docs, slot, qm is not None)
        call(kernel, qs + [kv], [], "add_block", flops=flops)

    def part(slot, q, qm, kv):
        out = jax.ShapeDtypeStruct((rows, (kv_heads * group_size + 2) * HD), jnp.bfloat16)
        return call(functools.partial(part_kernel, sizes, n_docs, slot), [q, qm, kv], [out], "mate_part")[0]

    def merge(parts):
        out = jax.ShapeDtypeStruct((rows, kv_heads * group_size * HD), jnp.bfloat16)
        return call(functools.partial(merge_kernel, sizes, mated), parts, [out], "merge", keeps=False)[0]

    def after(block):
        block, held[-1] = lax.optimization_barrier((block, held[-1]))
        return block

    return own, back, add, part, merge, after


def pack(keys, values, lengths, pack_order, table):
    rows, width = keys.shape
    n_docs = lengths.shape[0]
    hbm = pl.BlockSpec(memory_space=pltpu.HBM)
    scalars = [lengths, pack_order] + ([] if table is None else [table])
    return pl.pallas_call(
        functools.partial(pack_kernel, rows, n_docs, table is not None),
        out_shape=[
            jax.ShapeDtypeStruct((rows, 2 * width), keys.dtype),
            INFO_SPACE((STARTS + n_docs,), jnp.int32),
        ],
        in_specs=[hbm] * (len(scalars) + 2),
        out_specs=[pl.BlockSpec(memory_space=pltpu.VMEM), pl.BlockSpec(memory_space=pltpu.SMEM)],
        scratch_shapes=[
            pltpu.VMEM((rows, width), values.dtype),
            pltpu.SMEM((n_docs,), jnp.int32),
            pltpu.SMEM((n_docs,), jnp.int32),
            pltpu.SMEM((1 + 2 * SLOTS,), jnp.int32),
            pltpu.SemaphoreType.DMA((5,)),
        ],
        name="pack_keys_values",
    )(*scalars, keys, values)


def ring_shards(groups, queries, keys, values, lengths, pack_order):
    rows, kv_heads = queries.shape[0], keys.shape[1] // HD
    m = len(RING)
    sizes = (kv_heads, queries.shape[1] // keys.shape[1], rows)
    route, user = make_plan(groups, FIRST // rows)
    mate_of = [d if d < 2 * m else d ^ m for d in range(groups * m)]
    table = jnp.array([[mate] + row for mate, row in zip(mate_of, block_table(route, user, groups))], jnp.int32)
    kv, info = pack(keys, values, lengths, pack_order, table)
    own, back, add, part, merge, after = calls(sizes, lengths.shape[0], info, True)

    def send(block, op, step):
        return lax.ppermute(block, AXES, sorted((e, d) for d, (e, _) in route[op, step].items()))

    mates = [(d, d ^ m) for d in range(2 * m, groups * m)]
    eight_back = [(m + i, 3 * m + i) for i in range(m)] + [(2 * m + i, 2 * m + i) for i in range(m)]
    a1 = send(kv, "A", 1)
    q = queries
    own(q, kv)
    b1 = send(kv, "B", 1)
    qm = lax.ppermute(q, AXES, mates)
    kv8 = lax.ppermute(kv, AXES, eight_back)
    a2 = send(after(a1), "A", 2)
    back(7, qm, kv8)
    add(0, q, qm, a1)
    b2 = send(after(b1), "B", 2)
    add(1, q, qm, b1)
    a3 = send(after(a2), "A", 3)
    add(2, q, qm, a2)
    b3 = send(after(b2), "B", 3)
    add(3, q, qm, b2)
    a4 = send(after(a3), "A", 4)
    add(4, q, qm, a3)
    mine = part(5, q, qm, b3)
    theirs = lax.ppermute(mine, AXES, mates)
    add(6, q, None, a4, LAST_FLOPS)
    return merge([theirs])


def chain_shards(queries, keys, values, lengths, pack_order):
    rows, kv_heads = queries.shape[0], keys.shape[1] // HD
    sizes = (kv_heads, queries.shape[1] // keys.shape[1], rows)
    n = lax.axis_size(AXES)
    kv, info = pack(keys, values, lengths, pack_order, None)
    own, back, add, part, merge, after = calls(sizes, lengths.shape[0], info, False)
    q = queries
    own(q, kv)
    for hop in range(HOPS):
        kv = lax.ppermute(kv, AXES, [(d, d + 1) for d in range(n - 1)])
        add(hop, q, None, kv)
    return merge([])


def solution(mesh):
    spec, whole = P(AXES, None), P()
    outer, inner = mesh.shape["outer"], mesh.shape["inner"]
    ring = outer == 4 and inner == len(RING) == HOPS
    shards = functools.partial(ring_shards, outer) if ring else chain_shards
    return jax.shard_map(
        shards, mesh=mesh, in_specs=(spec, spec, spec, whole, whole), out_specs=spec, check_vma=False
    )
```

```python
import functools
import math

import jax
import jax.numpy as jnp
from jax import lax
from jax.experimental import pallas as pl
from jax.experimental.pallas import tpu as pltpu
from jax.sharding import PartitionSpec as P

HD = 128
HOPS = 8
FIRST = 1024
AXES = ("outer", "inner")
NEG = -1e30
SCALE = math.log2(math.e) / math.sqrt(HD)
RING = (0, 2, 4, 6, 7, 5, 3, 1)
OWN, MATE, NONE = 0, 1, 2
VMEM_LIMIT = 40 * 1024 * 1024
SLOTS = 10
STARTS = 2 + 2 * SLOTS
FLOPS = 1000
LAST_FLOPS = 50_000_000_000


def make_plan(groups, first_blocks):
    m = len(RING)
    n = groups * m
    place = {j: p for p, j in enumerate(RING)}

    def held(chip, odd, j):
        x, i = divmod(chip, m)
        o = 2 * x + odd
        if odd and j > i and (i, j) != (0, 1):
            o = (o + 2) % groups
        return o * m + j

    straight = [(n - m + 2, n - m + 3), (n - m + 3, n - m + 4), (n - 3 * m + 1, n - 2 * m)]

    def uses(q, b):
        return 0 < q - b <= HOPS and not (b < first_blocks <= q) and (b, q) not in straight

    def user(d, b):
        return d if uses(d, b) else d ^ m if uses(d ^ m, b) else None

    ops = [("own", 1), ("mate", 1), ("own", 2), ("mate", 2), ("own", 3), ("mate", 3), ("own", 4)]
    route = {}
    for op, s in ops:
        route[op, s] = {}
        for d in range(n):
            o, i = divmod(d, m)
            x, core = divmod(o, 2)
            odd = core if op == "own" else 1 - core
            way = 1 if core else -1
            j = RING[(place[i] - way * s) % m]
            b = held(x * m + i, odd, j)
            behind = RING[(place[i] - way) % m]
            (source,) = [
                (2 * y + core) * m + behind for y in range(groups // 2) if held(y * m + behind, odd, j) == b
            ]
            route[op, s][d] = (source, b)
    for op, s in reversed(ops):
        sends_on = {e for e, _ in route.get((op, s + 1), {}).values()}
        route[op, s] = {d: r for d, r in route[op, s].items() if user(d, r[1]) is not None or d in sends_on}
    route["own", 4] = {user(d, b): (e, b) for d, (e, b) in route["own", 4].items()}
    return route, user, straight


def block_table(route, user, straight, groups):
    m = len(RING)
    rows = []
    for d in range(groups * m):
        row = [d ^ m]
        for key in [("own", 1), ("mate", 1), ("own", 2), ("mate", 2), ("own", 3), ("mate", 3), ("own", 4)]:
            if d not in route[key]:
                row += [0, NONE]
                continue
            b = route[key][d][1]
            u = d if key == ("own", 4) else user(d, b)
            row += [b, NONE if u is None else OWN if u == d else MATE]
        row += [d ^ m, OWN if user(d, d ^ m) == d else NONE]
        o = d // m
        row += [d - m, OWN] if o % 2 == 0 and o > 0 else [0, NONE]
        row += [x for b, q in straight if q == d for x in (b, OWN)] or [0, NONE]
        rows.append(row)
    return rows


def position(axes):
    outer, inner = axes
    return lax.axis_index(outer) * lax.axis_size(inner) + lax.axis_index(inner)


def attend_block(sizes, q_of, kv_ref, bias, state, u, fresh):
    kv_heads, group_size, _ = sizes
    acc_ref, max_ref, sum_ref = state
    tile = 2 if group_size % 2 == 0 else 1
    bias = jnp.concatenate([bias] * tile, axis=1)
    for g in range(kv_heads):
        keys = kv_ref[:, g * HD : (g + 1) * HD]
        values = kv_ref[:, (kv_heads + g) * HD : (kv_heads + g + 1) * HD]
        for j in range(0, group_size, tile):
            columns = slice(j * HD, (j + tile) * HD)
            queries = jnp.concatenate([q_of(g * group_size + j + k) for k in range(tile)], axis=0)
            s = lax.dot_general(keys, queries, (((1,), (1,)), ((), ())), preferred_element_type=jnp.float32)
            s = s * SCALE + bias
            top = jnp.max(s, axis=0, keepdims=True)
            if not fresh:
                old = max_ref[u, g, :, columns]
                top = jnp.maximum(old, top)
                fade = jnp.exp2(old - top)
            p = jnp.exp2(s - top)
            total = jnp.sum(p, axis=0, keepdims=True)
            mixed = jnp.dot(values, p.astype(jnp.bfloat16), preferred_element_type=jnp.float32)
            max_ref[u, g, :, columns] = top
            sum_ref[u, g, :, columns] = total if fresh else sum_ref[u, g, :, columns] * fade + total
            acc_ref[u, g, :, columns] = mixed if fresh else acc_ref[u, g, :, columns] * fade + mixed


def head_of(ref):
    return lambda h: ref[:, h * HD : (h + 1) * HD]


def mask_bias(info_ref, n_docs, query_base, key_base, rows):
    query_pos = query_base + lax.broadcasted_iota(jnp.int32, (8, rows), 1)

    def latest(j, seen):
        start = info_ref[STARTS + j]
        return jnp.where(start <= query_pos, start, seen)

    seen = lax.fori_loop(0, n_docs, latest, jnp.zeros((8, rows), jnp.int32), unroll=n_docs <= 8)
    seen, query_pos = (jnp.concatenate([x] * (rows // 8), axis=0) for x in (seen, query_pos))
    key_pos = key_base + lax.broadcasted_iota(jnp.int32, (rows, rows), 0)
    return jnp.where((key_pos >= seen) & (key_pos <= query_pos), 0.0, NEG).astype(jnp.float32)


def pack_kernel(rows, n_docs, table, *refs):
    *far, k_ref, v_ref, kv_ref, info_ref, v_here, lengths_ref, order_ref, row_ref, sems = refs
    width = k_ref.shape[1]
    device = position(AXES)
    fetch_v = pltpu.make_async_copy(v_ref, v_here, sems.at[0])
    fetch_k = pltpu.make_async_copy(k_ref, kv_ref.at[:, pl.ds(0, width)], sems.at[1])
    small = [(far[0], lengths_ref), (far[1], order_ref)] + ([(far[2].at[device], row_ref)] if table else [])
    fetches = [pltpu.make_async_copy(a, b, sems.at[2 + k]) for k, (a, b) in enumerate(small)]
    for fetch in [fetch_v, fetch_k, *fetches]:
        fetch.start()
    for fetch in fetches:
        fetch.wait()

    mate = row_ref[0] if table else device
    info_ref[0] = device
    info_ref[1] = mate
    own_first, mate_first = device * rows, mate * rows

    def document(j, carry):
        start, own_seen, mate_seen = carry
        info_ref[STARTS + j] = start
        own_seen = jnp.where(start <= own_first, start, own_seen)
        mate_seen = jnp.where(start <= mate_first, start, mate_seen)
        return start + lengths_ref[order_ref[j]], own_seen, mate_seen

    zero = jnp.int32(0)
    _, own_seen, mate_seen = lax.fori_loop(0, n_docs, document, (zero, zero, zero), unroll=n_docs <= 8)
    for slot in range(SLOTS):
        if table:
            block, use = row_ref[1 + 2 * slot], row_ref[2 + 2 * slot]
        else:
            block, use = device - 1 - slot, OWN
        seen = jnp.where(use == OWN, own_seen, mate_seen)
        shown = (block >= 0) & (block * rows + rows > seen)
        info_ref[2 + 2 * slot] = block
        info_ref[3 + 2 * slot] = jnp.where(shown, use, NONE)

    fetch_v.wait()
    for g in range(width // HD):
        kv_ref[:, width + g * HD : width + (g + 1) * HD] = v_here[:, g * HD : (g + 1) * HD].T
    fetch_k.wait()


def fetch_kernel(q_ref, here_ref, sem):
    fetch = pltpu.make_async_copy(q_ref, here_ref, sem)
    fetch.start()
    fetch.wait()


def fetched(queries):
    return pl.pallas_call(
        fetch_kernel,
        out_shape=pltpu.VMEM(queries.shape, queries.dtype),
        in_specs=[pl.BlockSpec(memory_space=pltpu.HBM)],
        out_specs=pl.BlockSpec(memory_space=pltpu.VMEM),
        scratch_shapes=[pltpu.SemaphoreType.DMA],
        name="fetch_queries",
    )(queries)


def own_kernel(sizes, n_docs, info_ref, q_ref, kv_ref, *state):
    rows = sizes[2]
    base = info_ref[0] * rows
    bias = mask_bias(info_ref, n_docs, base, base, rows)
    attend_block(sizes, head_of(q_ref), kv_ref, bias, state, OWN, True)
    if state[0].shape[0] > 1:
        for ref, value in zip(state, (0.0, NEG, 0.0)):
            ref[MATE] = jnp.full(ref.shape[1:], value, jnp.float32)


def add_block(sizes, n_docs, slot, info_ref, q_ref, qm_ref, kv_ref, state):
    rows = sizes[2]
    use = info_ref[3 + 2 * slot]

    @pl.when(use != NONE)
    def _():
        mine = use == OWN
        query_base = jnp.where(mine, info_ref[0], info_ref[1]) * rows
        bias = mask_bias(info_ref, n_docs, query_base, info_ref[2 + 2 * slot] * rows, rows)
        q_of = head_of(q_ref)
        if qm_ref is not None:
            q_own, q_mate = q_of, head_of(qm_ref)
            q_of = lambda h: jnp.where(mine, q_own(h), q_mate(h))
        attend_block(sizes, q_of, kv_ref, bias, state, use, False)


def add_kernel(sizes, n_docs, slot, mated, info_ref, q_ref, *refs):
    qm_ref, refs = (refs[0], refs[1:]) if mated else (None, refs)
    add_block(sizes, n_docs, slot, info_ref, q_ref, qm_ref, refs[0], refs[4:])


def split3(x):
    a = x.astype(jnp.bfloat16)
    rest = x - a.astype(jnp.float32)
    b = rest.astype(jnp.bfloat16)
    return a, b, (rest - b.astype(jnp.float32)).astype(jnp.bfloat16)


def part_kernel(sizes, n_docs, slot, info_ref, q_ref, qm_ref, kv_ref, a_in, m_in, s_in, part_ref, *state):
    kv_heads, group_size, rows = sizes
    add_block(sizes, n_docs, slot, info_ref, q_ref, qm_ref, kv_ref, state)
    acc_ref, max_ref, sum_ref = state
    width = group_size * HD
    heads = kv_heads * group_size
    tops, sums = [], []
    for g in range(kv_heads):
        top, total = max_ref[MATE, g], sum_ref[MATE, g]
        share = 1.0 / jnp.where(total > 0, total, 1.0)
        part_ref[:, g * width : (g + 1) * width] = (acc_ref[MATE, g] * share).astype(jnp.bfloat16)
        for j in range(group_size):
            tops.append(top[:, j * HD : (j + 1) * HD])
            sums.append(total[:, j * HD : (j + 1) * HD])
    for column, stats in enumerate((tops, sums)):
        place = (heads + column) * HD
        for k, piece in enumerate(split3(jnp.concatenate(stats, axis=0))):
            part_ref[k * heads : (k + 1) * heads, place : place + HD] = piece


def merge_kernel(sizes, mated, info_ref, *refs):
    kv_heads, group_size, rows = sizes
    heads = kv_heads * group_size
    part_ref, refs = (refs[0], refs[1:]) if mated else (None, refs)
    acc_ref, max_ref, sum_ref, out_ref = refs
    if mated:
        tops, sums = (
            sum(part_ref[k * heads : (k + 1) * heads, c * HD : (c + 1) * HD].astype(jnp.float32) for k in range(3))
            for c in (heads, heads + 1)
        )
        met = info_ref[1] != info_ref[0]
        tops, sums = jnp.where(met, tops, NEG), jnp.where(met, sums, 0.0)
    for g in range(kv_heads):
        for j in range(group_size):
            h, mine = g * group_size + j, slice(j * HD, (j + 1) * HD)
            numer, top, total = acc_ref[OWN, g, :, mine], max_ref[OWN, g, :, mine], sum_ref[OWN, g, :, mine]
            if mated:
                both = jnp.maximum(top, tops[h : h + 1])
                weight, other = jnp.exp2(top - both), jnp.exp2(tops[h : h + 1] - both) * sums[h : h + 1]
                share = 1.0 / (total * weight + other)
                theirs = jnp.where(met, part_ref[:, h * HD : (h + 1) * HD].astype(jnp.float32), 0.0)
                out = numer * (weight * share) + theirs * (other * share)
            else:
                out = numer * (1.0 / total)
            out_ref[:, h * HD : (h + 1) * HD] = out.astype(jnp.bfloat16).T


def calls(sizes, n_docs, info, mated):
    kv_heads, group_size, rows = sizes
    tall = group_size * rows
    sets = 2 if mated else 1
    state = [
        pltpu.VMEM((sets, kv_heads, HD, tall), jnp.float32),
        pltpu.VMEM((sets, kv_heads, 1, tall), jnp.float32),
        pltpu.VMEM((sets, kv_heads, 1, tall), jnp.float32),
    ]
    smem, vmem = pl.BlockSpec(memory_space=pltpu.SMEM), pl.BlockSpec(memory_space=pltpu.VMEM)
    held = []

    def call(kernel, arrays, out, name, keeps=True, flops=FLOPS):
        n_in = 1 + len(arrays)
        out = out + (state if keeps else [])
        result = pl.pallas_call(
            kernel,
            out_shape=out,
            in_specs=[smem] + [vmem] * (len(arrays) + len(held)),
            out_specs=[vmem] * len(out),
            input_output_aliases={n_in + k: len(out) - 3 + k for k in range(len(held))} if keeps else {},
            compiler_params=pltpu.CompilerParams(vmem_limit_bytes=VMEM_LIMIT),
            cost_estimate=pl.CostEstimate(flops=flops, bytes_accessed=1024, transcendentals=0),
            name=name,
        )(info, *arrays, *held)
        if not keeps:
            return result
        held[:] = result[-3:]
        return result[:-3]

    def own(q, kv):
        call(functools.partial(own_kernel, sizes, n_docs), [q, kv], [], "own_block")

    def add(slot, q, qm, kv, flops=FLOPS):
        qs = [q] if qm is None else [q, qm]
        kernel = functools.partial(add_kernel, sizes, n_docs, slot, qm is not None)
        call(kernel, qs + [kv], [], "add_block", flops=flops)

    def part(slot, q, qm, kv):
        out = jax.ShapeDtypeStruct((rows, (kv_heads * group_size + 2) * HD), jnp.bfloat16)
        return call(functools.partial(part_kernel, sizes, n_docs, slot), [q, qm, kv], [out], "mate_part")[0]

    def merge(parts):
        out = jax.ShapeDtypeStruct((rows, kv_heads * group_size * HD), jnp.bfloat16)
        return call(functools.partial(merge_kernel, sizes, mated), parts, [out], "merge", keeps=False)[0]

    def after(block):
        block, held[-1] = lax.optimization_barrier((block, held[-1]))
        return block

    return own, add, part, merge, after


def pack(keys, values, lengths, pack_order, table):
    rows, width = keys.shape
    n_docs = lengths.shape[0]
    hbm = pl.BlockSpec(memory_space=pltpu.HBM)
    scalars = [lengths, pack_order] + ([] if table is None else [table])
    return pl.pallas_call(
        functools.partial(pack_kernel, rows, n_docs, table is not None),
        out_shape=[
            pltpu.VMEM((rows, 2 * width), keys.dtype),
            pltpu.SMEM((STARTS + n_docs,), jnp.int32),
        ],
        in_specs=[hbm] * (len(scalars) + 2),
        out_specs=[pl.BlockSpec(memory_space=pltpu.VMEM), pl.BlockSpec(memory_space=pltpu.SMEM)],
        scratch_shapes=[
            pltpu.VMEM((rows, width), values.dtype),
            pltpu.SMEM((n_docs,), jnp.int32),
            pltpu.SMEM((n_docs,), jnp.int32),
            pltpu.SMEM((1 + 2 * SLOTS,), jnp.int32),
            pltpu.SemaphoreType.DMA((5,)),
        ],
        name="pack_keys_values",
    )(*scalars, keys, values)


def ring_shards(groups, queries, keys, values, lengths, pack_order):
    rows, kv_heads = queries.shape[0], keys.shape[1] // HD
    m = len(RING)
    sizes = (kv_heads, queries.shape[1] // keys.shape[1], rows)
    route, user, straight = make_plan(groups, FIRST // rows)
    table = jnp.array(block_table(route, user, straight, groups), jnp.int32)
    kv, info = pack(keys, values, lengths, pack_order, table)
    own, add, part, merge, after = calls(sizes, lengths.shape[0], info, True)

    def send(block, op, step):
        return lax.ppermute(block, AXES, sorted((e, d) for d, (e, _) in route[op, step].items()))

    mates = [(d, d ^ m) for d in range(groups * m)]
    eight_back = [(d - m, d) for o in range(2, groups, 2) for d in range(o * m, (o + 1) * m)]
    u1 = send(kv, "own", 1)
    kvm = lax.ppermute(kv, AXES, mates)
    q = fetched(queries)
    own(q, kv)
    w1 = send(after(kvm), "mate", 1)
    qm = lax.ppermute(queries, AXES, mates)
    kv1 = lax.ppermute(kv, AXES, straight)
    u2 = send(after(u1), "own", 2)
    add(7, q, None, kvm)
    add(0, q, qm, u1)
    w2 = send(after(w1), "mate", 2)
    add(1, q, qm, w1)
    add(9, q, None, kv1)
    kv8 = lax.ppermute(after(kv), AXES, eight_back)
    u3 = send(after(u2), "own", 3)
    add(2, q, qm, u2)
    w3 = send(after(w2), "mate", 3)
    add(3, q, qm, w2)
    add(8, q, None, kv8)
    u4 = send(after(u3), "own", 4)
    add(4, q, qm, u3)
    mine = part(5, q, qm, w3)
    theirs = lax.ppermute(mine, AXES, mates)
    add(6, q, None, u4, LAST_FLOPS)
    return merge([theirs])


def chain_shards(queries, keys, values, lengths, pack_order):
    rows, kv_heads = queries.shape[0], keys.shape[1] // HD
    sizes = (kv_heads, queries.shape[1] // keys.shape[1], rows)
    n = lax.axis_size(AXES)
    kv, info = pack(keys, values, lengths, pack_order, None)
    own, add, part, merge, after = calls(sizes, lengths.shape[0], info, False)
    q = queries
    own(q, kv)
    for hop in range(HOPS):
        kv = lax.ppermute(kv, AXES, [(d, d + 1) for d in range(n - 1)])
        add(hop, q, None, kv)
    return merge([])


def solution(mesh):
    spec, whole = P(AXES, None), P()
    outer, inner = mesh.shape["outer"], mesh.shape["inner"]
    ring = outer == 4 and inner == len(RING) == HOPS
    shards = functools.partial(ring_shards, outer) if ring else chain_shards
    return jax.shard_map(
        shards, mesh=mesh, in_specs=(spec, spec, spec, whole, whole), out_specs=spec, check_vma=False
    )
```

```python
import functools
import math

import jax
import jax.numpy as jnp
from jax import lax
from jax.experimental import pallas as pl
from jax.experimental.pallas import tpu as pltpu
from jax.sharding import PartitionSpec as P

HD = 128
HOPS = 8
FIRST = 1024
AXES = ("outer", "inner")
NEG = -1e30
SCALE = math.log2(math.e) / math.sqrt(HD)
RING = (0, 2, 4, 6, 7, 5, 3, 1)
OWN, MATE, NONE = 0, 1, 2
VMEM_LIMIT = 40 * 1024 * 1024
SLOTS = 12
STARTS = 2 + 2 * SLOTS
FLOPS = 1000
LAST_FLOPS = 50_000_000_000


def make_plan(groups, first_blocks):
    m = len(RING)
    n = groups * m
    place = {j: p for p, j in enumerate(RING)}

    def held(chip, odd, j):
        x, i = divmod(chip, m)
        o = 2 * x + odd
        if odd and j > i and (i, j) != (0, 1):
            o = (o + 2) % groups
        return o * m + j

    last = n - m
    straight = [
        (last + 2, last + 3, last + 2),
        (last + 3, last + 4, last - m + 5),
        (last - 2 * m + 1, last - m, last - 2 * m),
    ]

    def uses(q, b):
        return 0 < q - b <= HOPS and not (b < first_blocks <= q) and (b, q) not in [x[:2] for x in straight]

    def user(d, b):
        return d if uses(d, b) else d ^ m if uses(d ^ m, b) else None

    ops = [("own", 1), ("mate", 1), ("own", 2), ("mate", 2), ("own", 3), ("mate", 3), ("own", 4)]
    route = {}
    for op, s in ops:
        route[op, s] = {}
        for d in range(n):
            o, i = divmod(d, m)
            x, core = divmod(o, 2)
            odd = core if op == "own" else 1 - core
            way = 1 if core else -1
            j = RING[(place[i] - way * s) % m]
            b = held(x * m + i, odd, j)
            behind = RING[(place[i] - way) % m]
            (source,) = [
                (2 * y + core) * m + behind for y in range(groups // 2) if held(y * m + behind, odd, j) == b
            ]
            route[op, s][d] = (source, b)
    for op, s in reversed(ops):
        sends_on = {e for e, _ in route.get((op, s + 1), {}).values()}
        route[op, s] = {d: r for d, r in route[op, s].items() if user(d, r[1]) is not None or d in sends_on}
    route["own", 4] = {user(d, b): (e, b) for d, (e, b) in route["own", 4].items()}
    return route, user, straight


def block_table(route, user, straight, groups):
    m = len(RING)
    rows = []
    for d in range(groups * m):
        row = [d ^ m]
        for key in [("own", 1), ("mate", 1), ("own", 2), ("mate", 2), ("own", 3), ("mate", 3), ("own", 4)]:
            if d not in route[key]:
                row += [0, NONE]
                continue
            b = route[key][d][1]
            u = d if key == ("own", 4) else user(d, b)
            row += [b, NONE if u is None else OWN if u == d else MATE]
        row += [d ^ m, OWN if user(d, d ^ m) == d else NONE]
        o = d // m
        row += [d - m, OWN] if o % 2 == 0 and o > 0 else [0, NONE]
        for b, q, _ in straight:
            row += [b, OWN] if q == d else [0, NONE]
        rows.append(row)
    return rows


def position(axes):
    outer, inner = axes
    return lax.axis_index(outer) * lax.axis_size(inner) + lax.axis_index(inner)


def attend_block(sizes, q_of, kv_ref, bias, state, u, fresh, finish=None):
    kv_heads, group_size, _ = sizes
    acc_ref, max_ref, sum_ref = state
    tile = 2 if group_size % 2 == 0 else 1
    bias = jnp.concatenate([bias] * tile, axis=1)
    for g in range(kv_heads):
        keys = kv_ref[:, g * HD : (g + 1) * HD]
        values = kv_ref[:, (kv_heads + g) * HD : (kv_heads + g + 1) * HD]
        for j in range(0, group_size, tile):
            columns = slice(j * HD, (j + tile) * HD)
            queries = jnp.concatenate([q_of(g * group_size + j + k) for k in range(tile)], axis=0)
            s = lax.dot_general(keys, queries, (((1,), (1,)), ((), ())), preferred_element_type=jnp.float32)
            s = s * SCALE + bias
            top = jnp.max(s, axis=0, keepdims=True)
            if not fresh:
                old = max_ref[u, g, :, columns]
                top = jnp.maximum(old, top)
                fade = jnp.exp2(old - top)
            p = jnp.exp2(s - top)
            total = jnp.sum(p, axis=0, keepdims=True)
            mixed = jnp.dot(values, p.astype(jnp.bfloat16), preferred_element_type=jnp.float32)
            max_ref[u, g, :, columns] = top
            sum_ref[u, g, :, columns] = total if fresh else sum_ref[u, g, :, columns] * fade + total
            acc_ref[u, g, :, columns] = mixed if fresh else acc_ref[u, g, :, columns] * fade + mixed
        if finish is not None:
            finish(g)


def head_of(ref):
    return lambda h: ref[:, h * HD : (h + 1) * HD]


def mask_bias(info_ref, n_docs, query_base, key_base, rows):
    query_pos = query_base + lax.broadcasted_iota(jnp.int32, (8, rows), 1)

    def latest(j, seen):
        start = info_ref[STARTS + j]
        return jnp.where(start <= query_pos, start, seen)

    seen = lax.fori_loop(0, n_docs, latest, jnp.zeros((8, rows), jnp.int32), unroll=n_docs <= 8)
    seen, query_pos = (jnp.concatenate([x] * (rows // 8), axis=0) for x in (seen, query_pos))
    key_pos = key_base + lax.broadcasted_iota(jnp.int32, (rows, rows), 0)
    return jnp.where((key_pos >= seen) & (key_pos <= query_pos), 0.0, NEG).astype(jnp.float32)


def pack_kernel(rows, n_docs, table, *refs):
    *far, k_ref, v_ref, kv_ref, info_ref, v_here, lengths_ref, order_ref, row_ref, sems = refs
    width = k_ref.shape[1]
    device = position(AXES)
    fetch_v = pltpu.make_async_copy(v_ref, v_here, sems.at[0])
    fetch_k = pltpu.make_async_copy(k_ref, kv_ref.at[:, pl.ds(0, width)], sems.at[1])
    small = [(far[0], lengths_ref), (far[1], order_ref)] + ([(far[2].at[device], row_ref)] if table else [])
    fetches = [pltpu.make_async_copy(a, b, sems.at[2 + k]) for k, (a, b) in enumerate(small)]
    for fetch in [fetch_v, fetch_k, *fetches]:
        fetch.start()
    for fetch in fetches:
        fetch.wait()

    mate = row_ref[0] if table else device
    info_ref[0] = device
    info_ref[1] = mate
    own_first, mate_first = device * rows, mate * rows

    def document(j, carry):
        start, own_seen, mate_seen = carry
        info_ref[STARTS + j] = start
        own_seen = jnp.where(start <= own_first, start, own_seen)
        mate_seen = jnp.where(start <= mate_first, start, mate_seen)
        return start + lengths_ref[order_ref[j]], own_seen, mate_seen

    zero = jnp.int32(0)
    _, own_seen, mate_seen = lax.fori_loop(0, n_docs, document, (zero, zero, zero), unroll=n_docs <= 8)
    for slot in range(SLOTS):
        if table:
            block, use = row_ref[1 + 2 * slot], row_ref[2 + 2 * slot]
        else:
            block, use = device - 1 - slot, OWN
        seen = jnp.where(use == OWN, own_seen, mate_seen)
        shown = (block >= 0) & (block * rows + rows > seen)
        info_ref[2 + 2 * slot] = block
        info_ref[3 + 2 * slot] = jnp.where(shown, use, NONE)

    fetch_v.wait()
    for g in range(width // HD):
        kv_ref[:, width + g * HD : width + (g + 1) * HD] = v_here[:, g * HD : (g + 1) * HD].T
    fetch_k.wait()


def fetch_kernel(q_ref, here_ref, sem):
    fetch = pltpu.make_async_copy(q_ref, here_ref, sem)
    fetch.start()
    fetch.wait()


def fetched(queries):
    return pl.pallas_call(
        fetch_kernel,
        out_shape=pltpu.VMEM(queries.shape, queries.dtype),
        in_specs=[pl.BlockSpec(memory_space=pltpu.HBM)],
        out_specs=pl.BlockSpec(memory_space=pltpu.VMEM),
        scratch_shapes=[pltpu.SemaphoreType.DMA],
        name="fetch_queries",
    )(queries)


def own_kernel(sizes, n_docs, info_ref, q_ref, kv_ref, *state):
    rows = sizes[2]
    base = info_ref[0] * rows
    bias = mask_bias(info_ref, n_docs, base, base, rows)
    attend_block(sizes, head_of(q_ref), kv_ref, bias, state, OWN, True)
    if state[0].shape[0] > 1:
        for ref, value in zip(state, (0.0, NEG, 0.0)):
            ref[MATE] = jnp.full(ref.shape[1:], value, jnp.float32)


def add_block(sizes, n_docs, slot, info_ref, q_ref, qm_ref, kv_ref, state):
    rows = sizes[2]
    use = info_ref[3 + 2 * slot]

    @pl.when(use != NONE)
    def _():
        mine = use == OWN
        query_base = jnp.where(mine, info_ref[0], info_ref[1]) * rows
        bias = mask_bias(info_ref, n_docs, query_base, info_ref[2 + 2 * slot] * rows, rows)
        q_of = head_of(q_ref)
        if qm_ref is not None:
            q_own, q_mate = q_of, head_of(qm_ref)
            q_of = lambda h: jnp.where(mine, q_own(h), q_mate(h))
        attend_block(sizes, q_of, kv_ref, bias, state, use, False)


def add_kernel(sizes, n_docs, slot, mated, info_ref, q_ref, *refs):
    qm_ref, refs = (refs[0], refs[1:]) if mated else (None, refs)
    add_block(sizes, n_docs, slot, info_ref, q_ref, qm_ref, refs[0], refs[4:])


def split3(x):
    a = x.astype(jnp.bfloat16)
    rest = x - a.astype(jnp.float32)
    b = rest.astype(jnp.bfloat16)
    return a, b, (rest - b.astype(jnp.float32)).astype(jnp.bfloat16)


def part_kernel(sizes, n_docs, slot, info_ref, q_ref, qm_ref, kv_ref, a_in, m_in, s_in, part_ref, *state):
    kv_heads, group_size, rows = sizes
    add_block(sizes, n_docs, slot, info_ref, q_ref, qm_ref, kv_ref, state)
    acc_ref, max_ref, sum_ref = state
    width = group_size * HD
    heads = kv_heads * group_size
    tops, sums = [], []
    for g in range(kv_heads):
        top, total = max_ref[MATE, g], sum_ref[MATE, g]
        share = 1.0 / jnp.where(total > 0, total, 1.0)
        part_ref[:, g * width : (g + 1) * width] = (acc_ref[MATE, g] * share).astype(jnp.bfloat16)
        for j in range(group_size):
            tops.append(top[:, j * HD : (j + 1) * HD])
            sums.append(total[:, j * HD : (j + 1) * HD])
    for column, stats in enumerate((tops, sums)):
        place = (heads + column) * HD
        for k, piece in enumerate(split3(jnp.concatenate(stats, axis=0))):
            part_ref[k * heads : (k + 1) * heads, place : place + HD] = piece


def touch_kernel(info_ref, kv_ref, *refs):
    pass


def last_kernel(sizes, n_docs, slot, mated, info_ref, q_ref, *refs):
    kv_heads, group_size, rows = sizes
    heads = kv_heads * group_size
    width = group_size * HD
    part_ref, refs = (refs[0], refs[1:]) if mated else (None, refs)
    kv_ref, acc_ref, max_ref, sum_ref, out_ref, out_here, sems = refs
    if mated:
        tops, sums = (
            sum(part_ref[k * heads : (k + 1) * heads, c * HD : (c + 1) * HD].astype(jnp.float32) for k in range(3))
            for c in (heads, heads + 1)
        )

    def store(g):
        columns = pl.ds(g * width, width)
        return pltpu.make_async_copy(out_here.at[:, columns], out_ref.at[:, columns], sems.at[g])

    def finish(g):
        for j in range(group_size):
            h, mine = g * group_size + j, slice(j * HD, (j + 1) * HD)
            numer, top, total = acc_ref[OWN, g, :, mine], max_ref[OWN, g, :, mine], sum_ref[OWN, g, :, mine]
            if mated:
                both = jnp.maximum(top, tops[h : h + 1])
                weight, other = jnp.exp2(top - both), jnp.exp2(tops[h : h + 1] - both) * sums[h : h + 1]
                share = 1.0 / (total * weight + other)
                theirs = part_ref[:, h * HD : (h + 1) * HD].astype(jnp.float32)
                out = numer * (weight * share) + theirs * (other * share)
            else:
                out = numer * (1.0 / total)
            out_here[:, h * HD : (h + 1) * HD] = out.astype(jnp.bfloat16).T
        store(g).start()

    use = info_ref[3 + 2 * slot]

    @pl.when(use != NONE)
    def _():
        bias = mask_bias(info_ref, n_docs, info_ref[0] * rows, info_ref[2 + 2 * slot] * rows, rows)
        attend_block(sizes, head_of(q_ref), kv_ref, bias, (acc_ref, max_ref, sum_ref), OWN, False, finish)

    @pl.when(use == NONE)
    def _():
        for g in range(kv_heads):
            finish(g)

    for g in range(kv_heads):
        store(g).wait()


def calls(sizes, n_docs, info, mated):
    kv_heads, group_size, rows = sizes
    tall = group_size * rows
    sets = 2 if mated else 1
    state = [
        pltpu.VMEM((sets, kv_heads, HD, tall), jnp.float32),
        pltpu.VMEM((sets, kv_heads, 1, tall), jnp.float32),
        pltpu.VMEM((sets, kv_heads, 1, tall), jnp.float32),
    ]
    smem, vmem = pl.BlockSpec(memory_space=pltpu.SMEM), pl.BlockSpec(memory_space=pltpu.VMEM)
    held = []

    def call(kernel, arrays, out, name, keeps=True, flops=FLOPS):
        n_in = 1 + len(arrays)
        out = out + (state if keeps else [])
        result = pl.pallas_call(
            kernel,
            out_shape=out,
            in_specs=[smem] + [vmem] * (len(arrays) + len(held)),
            out_specs=[vmem] * len(out),
            input_output_aliases={n_in + k: len(out) - 3 + k for k in range(len(held))} if keeps else {},
            compiler_params=pltpu.CompilerParams(vmem_limit_bytes=VMEM_LIMIT),
            cost_estimate=pl.CostEstimate(flops=flops, bytes_accessed=1024, transcendentals=0),
            name=name,
        )(info, *arrays, *held)
        if not keeps:
            return result
        held[:] = result[-3:]
        return result[:-3]

    def own(q, kv):
        call(functools.partial(own_kernel, sizes, n_docs), [q, kv], [], "own_block")

    def add(slot, q, qm, kv):
        qs = [q] if qm is None else [q, qm]
        kernel = functools.partial(add_kernel, sizes, n_docs, slot, qm is not None)
        call(kernel, qs + [kv], [], "add_block")

    def part(slot, q, qm, kv):
        out = jax.ShapeDtypeStruct((rows, (kv_heads * group_size + 2) * HD), jnp.bfloat16)
        return call(functools.partial(part_kernel, sizes, n_docs, slot), [q, qm, kv], [out], "mate_part")[0]

    def touch(kv):
        call(touch_kernel, [kv], [], "last_block_here", flops=LAST_FLOPS)

    def last(slot, q, parts, kv):
        return pl.pallas_call(
            functools.partial(last_kernel, sizes, n_docs, slot, mated),
            out_shape=jax.ShapeDtypeStruct((rows, kv_heads * group_size * HD), jnp.bfloat16),
            in_specs=[smem] + [vmem] * (2 + len(parts) + len(held)),
            out_specs=pl.BlockSpec(memory_space=pltpu.HBM),
            scratch_shapes=[
                pltpu.VMEM((rows, kv_heads * group_size * HD), jnp.bfloat16),
                pltpu.SemaphoreType.DMA((kv_heads,)),
            ],
            compiler_params=pltpu.CompilerParams(vmem_limit_bytes=VMEM_LIMIT),
            name="last_block",
        )(info, q, *parts, kv, *held)

    def after(block):
        block, held[-1] = lax.optimization_barrier((block, held[-1]))
        return block

    return own, add, part, touch, last, after


def pack(keys, values, lengths, pack_order, table):
    rows, width = keys.shape
    n_docs = lengths.shape[0]
    hbm = pl.BlockSpec(memory_space=pltpu.HBM)
    scalars = [lengths, pack_order] + ([] if table is None else [table])
    return pl.pallas_call(
        functools.partial(pack_kernel, rows, n_docs, table is not None),
        out_shape=[
            pltpu.VMEM((rows, 2 * width), keys.dtype),
            pltpu.SMEM((STARTS + n_docs,), jnp.int32),
        ],
        in_specs=[hbm] * (len(scalars) + 2),
        out_specs=[pl.BlockSpec(memory_space=pltpu.VMEM), pl.BlockSpec(memory_space=pltpu.SMEM)],
        scratch_shapes=[
            pltpu.VMEM((rows, width), values.dtype),
            pltpu.SMEM((n_docs,), jnp.int32),
            pltpu.SMEM((n_docs,), jnp.int32),
            pltpu.SMEM((1 + 2 * SLOTS,), jnp.int32),
            pltpu.SemaphoreType.DMA((5,)),
        ],
        name="pack_keys_values",
    )(*scalars, keys, values)


def ring_shards(groups, queries, keys, values, lengths, pack_order):
    rows, kv_heads = queries.shape[0], keys.shape[1] // HD
    m = len(RING)
    sizes = (kv_heads, queries.shape[1] // keys.shape[1], rows)
    route, user, straight = make_plan(groups, FIRST // rows)
    table = jnp.array(block_table(route, user, straight, groups), jnp.int32)
    kv, info = pack(keys, values, lengths, pack_order, table)
    own, add, part, touch, last, after = calls(sizes, lengths.shape[0], info, True)

    def send(block, op, step):
        return lax.ppermute(block, AXES, sorted((e, d) for d, (e, _) in route[op, step].items()))

    mates = [(d, d ^ m) for d in range(groups * m)]
    eight_back = [(d - m, d) for o in range(2, groups, 2) for d in range(o * m, (o + 1) * m)]
    u1 = send(kv, "own", 1)
    kvm = lax.ppermute(kv, AXES, mates)
    q = fetched(queries)
    own(q, kv)
    w1 = send(after(kvm), "mate", 1)
    qm = lax.ppermute(queries, AXES, mates)
    beside = [[(e, q)] for _, q, e in straight]
    near = [lax.ppermute(kv, AXES, beside[0])]
    u2 = send(after(u1), "own", 2)
    add(7, q, None, kvm)
    add(0, q, qm, u1)
    w2 = send(after(w1), "mate", 2)
    add(1, q, qm, w1)
    add(9, q, None, near[0])
    near += [lax.ppermute(after(w1), AXES, beside[1]), lax.ppermute(u1, AXES, beside[2])]
    kv8 = lax.ppermute(after(kv), AXES, eight_back)
    u3 = send(after(u2), "own", 3)
    add(2, q, qm, u2)
    w3 = send(after(w2), "mate", 3)
    add(3, q, qm, w2)
    u4 = send(after(u3), "own", 4)
    add(4, q, qm, u3)
    add(10, q, None, near[1])
    add(11, q, None, near[2])
    mine = part(5, q, qm, w3)
    theirs = lax.ppermute(mine, AXES, mates)
    add(8, q, None, kv8)
    touch(u4)
    return last(6, q, [theirs], u4)


def chain_shards(queries, keys, values, lengths, pack_order):
    rows, kv_heads = queries.shape[0], keys.shape[1] // HD
    sizes = (kv_heads, queries.shape[1] // keys.shape[1], rows)
    n = lax.axis_size(AXES)
    kv, info = pack(keys, values, lengths, pack_order, None)
    own, add, part, touch, last, after = calls(sizes, lengths.shape[0], info, False)
    q = queries
    own(q, kv)
    for hop in range(HOPS):
        kv = lax.ppermute(kv, AXES, [(d, d + 1) for d in range(n - 1)])
        if hop < HOPS - 1:
            add(hop, q, None, kv)
    return last(HOPS - 1, q, [], kv)


def solution(mesh):
    spec, whole = P(AXES, None), P()
    outer, inner = mesh.shape["outer"], mesh.shape["inner"]
    ring = outer == 4 and inner == len(RING) == HOPS
    shards = functools.partial(ring_shards, outer) if ring else chain_shards
    return jax.shard_map(
        shards, mesh=mesh, in_specs=(spec, spec, spec, whole, whole), out_specs=spec, check_vma=False
    )
```

```python
import functools
import math

import jax
import jax.numpy as jnp
from jax import lax
from jax.experimental import pallas as pl
from jax.experimental.pallas import tpu as pltpu
from jax.sharding import PartitionSpec as P

HD = 128
HOPS = 8
FIRST = 1024
AXES = ("outer", "inner")
NEG = -1e30
SCALE = math.log2(math.e) / math.sqrt(HD)
RING = (0, 2, 4, 6, 7, 5, 3, 1)
OWN, MATE, NONE = 0, 1, 2
VMEM_LIMIT = 40 * 1024 * 1024
SLOTS = 12
STARTS = 2 + 2 * SLOTS
FLOPS = 1000
LAST_FLOPS = 50_000_000_000


def make_plan(groups, first_blocks):
    m = len(RING)
    n = groups * m
    place = {j: p for p, j in enumerate(RING)}

    def held(chip, odd, j):
        x, i = divmod(chip, m)
        o = 2 * x + odd
        if odd and j > i and (i, j) != (0, 1):
            o = (o + 2) % groups
        return o * m + j

    last = n - m
    straight = [
        (last + 2, last + 3, last + 2),
        (last + 3, last + 4, last - m + 5),
        (last - 2 * m + 1, last - m, last - 2 * m),
    ]

    def uses(q, b):
        return 0 < q - b <= HOPS and not (b < first_blocks <= q) and (b, q) not in [x[:2] for x in straight]

    def user(d, b):
        return d if uses(d, b) else d ^ m if uses(d ^ m, b) else None

    ops = [("own", 1), ("mate", 1), ("own", 2), ("mate", 2), ("own", 3), ("mate", 3), ("own", 4)]
    route = {}
    for op, s in ops:
        route[op, s] = {}
        for d in range(n):
            o, i = divmod(d, m)
            x, core = divmod(o, 2)
            odd = core if op == "own" else 1 - core
            way = 1 if core else -1
            j = RING[(place[i] - way * s) % m]
            b = held(x * m + i, odd, j)
            behind = RING[(place[i] - way) % m]
            (source,) = [
                (2 * y + core) * m + behind for y in range(groups // 2) if held(y * m + behind, odd, j) == b
            ]
            route[op, s][d] = (source, b)
    for op, s in reversed(ops):
        sends_on = {e for e, _ in route.get((op, s + 1), {}).values()}
        route[op, s] = {d: r for d, r in route[op, s].items() if user(d, r[1]) is not None or d in sends_on}
    route["own", 4] = {user(d, b): (e, b) for d, (e, b) in route["own", 4].items()}
    return route, user, straight


def block_table(route, user, straight, groups):
    m = len(RING)
    rows = []
    for d in range(groups * m):
        row = [d ^ m]
        for key in [("own", 1), ("mate", 1), ("own", 2), ("mate", 2), ("own", 3), ("mate", 3), ("own", 4)]:
            if d not in route[key]:
                row += [0, NONE]
                continue
            b = route[key][d][1]
            u = d if key == ("own", 4) else user(d, b)
            row += [b, NONE if u is None else OWN if u == d else MATE]
        row += [d ^ m, OWN if user(d, d ^ m) == d else NONE]
        o = d // m
        back = [d - m, OWN] if o % 2 == 0 and o > 0 else [0, NONE]
        early = d % m in (3, 4)
        row += [0, NONE] if early else back
        for b, q, e in straight:
            row += [b, OWN] if q == d else back if early and b == e else [0, NONE]
        rows.append(row)
    return rows


def position(axes):
    outer, inner = axes
    return lax.axis_index(outer) * lax.axis_size(inner) + lax.axis_index(inner)


def attend_block(sizes, q_of, kv_ref, bias, state, u, fresh, finish=None):
    kv_heads, group_size, _ = sizes
    acc_ref, max_ref, sum_ref = state
    tile = 2 if group_size % 2 == 0 else 1
    bias = jnp.concatenate([bias] * tile, axis=1)
    for g in range(kv_heads):
        row = slice(g, g + 1)
        keys = kv_ref[:, g * HD : (g + 1) * HD]
        values = kv_ref[:, (kv_heads + g) * HD : (kv_heads + g + 1) * HD]
        for j in range(0, group_size, tile):
            columns = slice(j * HD, (j + tile) * HD)
            queries = jnp.concatenate([q_of(g * group_size + j + k) for k in range(tile)], axis=0)
            s = lax.dot_general(keys, queries, (((1,), (1,)), ((), ())), preferred_element_type=jnp.float32)
            s = s * SCALE + bias
            top = jnp.max(s, axis=0, keepdims=True)
            if not fresh:
                old = max_ref[u, row, columns]
                top = jnp.maximum(old, top)
                fade = jnp.exp2(old - top)
            p = jnp.exp2(s - top)
            total = jnp.sum(p, axis=0, keepdims=True)
            mixed = jnp.dot(values, p.astype(jnp.bfloat16), preferred_element_type=jnp.float32)
            max_ref[u, row, columns] = top
            sum_ref[u, row, columns] = total if fresh else sum_ref[u, row, columns] * fade + total
            acc_ref[u, g, :, columns] = mixed if fresh else acc_ref[u, g, :, columns] * fade + mixed
        if finish is not None and (g + 1) % (kv_heads // 2) == 0:
            finish(slice(g + 1 - kv_heads // 2, g + 1))


def head_of(ref):
    return lambda h: ref[:, h * HD : (h + 1) * HD]


def mask_bias(info_ref, n_docs, query_base, key_base, rows):
    query_pos = query_base + lax.broadcasted_iota(jnp.int32, (8, rows), 1)

    def latest(j, seen):
        start = info_ref[STARTS + j]
        return jnp.where(start <= query_pos, start, seen)

    seen = lax.fori_loop(0, n_docs, latest, jnp.zeros((8, rows), jnp.int32), unroll=n_docs <= 8)
    seen, query_pos = (jnp.concatenate([x] * (rows // 8), axis=0) for x in (seen, query_pos))
    key_pos = key_base + lax.broadcasted_iota(jnp.int32, (rows, rows), 0)
    return jnp.where((key_pos >= seen) & (key_pos <= query_pos), 0.0, NEG).astype(jnp.float32)


def pack_kernel(rows, n_docs, table, *refs):
    *far, k_ref, v_ref, kv_ref, info_ref, v_here, lengths_ref, order_ref, row_ref, sems = refs
    width = k_ref.shape[1]
    device = position(AXES)
    fetch_v = pltpu.make_async_copy(v_ref, v_here, sems.at[0])
    fetch_k = pltpu.make_async_copy(k_ref, kv_ref.at[:, pl.ds(0, width)], sems.at[1])
    small = [(far[0], lengths_ref), (far[1], order_ref)] + ([(far[2].at[device], row_ref)] if table else [])
    fetches = [pltpu.make_async_copy(a, b, sems.at[2 + k]) for k, (a, b) in enumerate(small)]
    for fetch in [fetch_v, fetch_k, *fetches]:
        fetch.start()
    for fetch in fetches:
        fetch.wait()

    mate = row_ref[0] if table else device
    info_ref[0] = device
    info_ref[1] = mate
    own_first, mate_first = device * rows, mate * rows

    def document(j, carry):
        start, own_seen, mate_seen = carry
        info_ref[STARTS + j] = start
        own_seen = jnp.where(start <= own_first, start, own_seen)
        mate_seen = jnp.where(start <= mate_first, start, mate_seen)
        return start + lengths_ref[order_ref[j]], own_seen, mate_seen

    zero = jnp.int32(0)
    _, own_seen, mate_seen = lax.fori_loop(0, n_docs, document, (zero, zero, zero), unroll=n_docs <= 8)
    for slot in range(SLOTS):
        if table:
            block, use = row_ref[1 + 2 * slot], row_ref[2 + 2 * slot]
        else:
            block, use = device - 1 - slot, OWN
        seen = jnp.where(use == OWN, own_seen, mate_seen)
        shown = (block >= 0) & (block * rows + rows > seen)
        info_ref[2 + 2 * slot] = block
        info_ref[3 + 2 * slot] = jnp.where(shown, use, NONE)

    fetch_v.wait()
    for g in range(width // HD):
        kv_ref[:, width + g * HD : width + (g + 1) * HD] = v_here[:, g * HD : (g + 1) * HD].T
    fetch_k.wait()


def fetch_kernel(q_ref, here_ref, sem):
    fetch = pltpu.make_async_copy(q_ref, here_ref, sem)
    fetch.start()
    fetch.wait()


def fetched(queries):
    return pl.pallas_call(
        fetch_kernel,
        out_shape=pltpu.VMEM(queries.shape, queries.dtype),
        in_specs=[pl.BlockSpec(memory_space=pltpu.HBM)],
        out_specs=pl.BlockSpec(memory_space=pltpu.VMEM),
        scratch_shapes=[pltpu.SemaphoreType.DMA],
        name="fetch_queries",
    )(queries)


def own_kernel(sizes, n_docs, info_ref, q_ref, kv_ref, *state):
    rows = sizes[2]
    base = info_ref[0] * rows
    bias = mask_bias(info_ref, n_docs, base, base, rows)
    attend_block(sizes, head_of(q_ref), kv_ref, bias, state, OWN, True)
    if state[0].shape[0] > 1:
        for ref, value in zip(state, (0.0, NEG, 0.0)):
            ref[MATE] = jnp.full(ref.shape[1:], value, jnp.float32)


def add_block(sizes, n_docs, slot, info_ref, q_ref, qm_ref, kv_ref, state):
    rows = sizes[2]
    use = info_ref[3 + 2 * slot]

    @pl.when(use != NONE)
    def _():
        mine = use == OWN
        query_base = jnp.where(mine, info_ref[0], info_ref[1]) * rows
        bias = mask_bias(info_ref, n_docs, query_base, info_ref[2 + 2 * slot] * rows, rows)
        q_of = head_of(q_ref)
        if qm_ref is not None:
            q_own, q_mate = q_of, head_of(qm_ref)
            q_of = lambda h: jnp.where(mine, q_own(h), q_mate(h))
        attend_block(sizes, q_of, kv_ref, bias, state, use, False)


def add_kernel(sizes, n_docs, slot, mated, info_ref, q_ref, *refs):
    qm_ref, refs = (refs[0], refs[1:]) if mated else (None, refs)
    add_block(sizes, n_docs, slot, info_ref, q_ref, qm_ref, refs[0], refs[4:])


def split3(x):
    a = x.astype(jnp.bfloat16)
    rest = x - a.astype(jnp.float32)
    b = rest.astype(jnp.bfloat16)
    return a, b, (rest - b.astype(jnp.float32)).astype(jnp.bfloat16)


def part_kernel(sizes, n_docs, slot, info_ref, q_ref, qm_ref, kv_ref, a_in, m_in, s_in, part_ref, *state):
    kv_heads, group_size, rows = sizes
    add_block(sizes, n_docs, slot, info_ref, q_ref, qm_ref, kv_ref, state)
    acc_ref, max_ref, sum_ref = state
    width = group_size * HD
    totals = sum_ref[MATE]
    shares = 1.0 / jnp.where(totals > 0, totals, 1.0)
    for g in range(kv_heads):
        part_ref[:, g * width : (g + 1) * width] = (acc_ref[MATE, g] * shares[g : g + 1]).astype(jnp.bfloat16)
    stats = jnp.concatenate([max_ref[MATE], totals], axis=0)
    for k, piece in enumerate(split3(stats)):
        part_ref[2 * k * kv_heads : 2 * (k + 1) * kv_heads, kv_heads * width :] = piece


def touch_kernel(info_ref, kv_ref, *refs):
    pass


def last_kernel(sizes, n_docs, slot, mated, info_ref, q_ref, *refs):
    kv_heads, group_size, rows = sizes
    width = group_size * HD
    part_ref, refs = (refs[0], refs[1:]) if mated else (None, refs)
    kv_ref, acc_ref, max_ref, sum_ref, out_ref, out_here, sems = refs
    if mated:
        stats = sum(
            part_ref[2 * k * kv_heads : 2 * (k + 1) * kv_heads, kv_heads * width :].astype(jnp.float32) for k in range(3)
        )
        tops, sums = stats[:kv_heads], stats[kv_heads:]

    def store(g):
        columns = pl.ds(g * width, width)
        return pltpu.make_async_copy(out_here.at[:, columns], out_ref.at[:, columns], sems.at[g])

    def finish(some):
        top, total = max_ref[OWN, some], sum_ref[OWN, some]
        if mated:
            both = jnp.maximum(top, tops[some])
            weight, other = jnp.exp2(top - both), jnp.exp2(tops[some] - both) * sums[some]
            share = 1.0 / (total * weight + other)
            mine, others = weight * share, other * share
        else:
            mine = 1.0 / total
        for k, g in enumerate(range(some.start, some.stop)):
            out = acc_ref[OWN, g] * mine[k : k + 1]
            if mated:
                theirs = part_ref[:, g * width : (g + 1) * width].astype(jnp.float32)
                out = out + theirs * others[k : k + 1]
            out = out.astype(jnp.bfloat16)
            for j in range(group_size):
                h = g * group_size + j
                out_here[:, h * HD : (h + 1) * HD] = out[:, j * HD : (j + 1) * HD].T
            store(g).start()

    use = info_ref[3 + 2 * slot]

    @pl.when(use != NONE)
    def _():
        bias = mask_bias(info_ref, n_docs, info_ref[0] * rows, info_ref[2 + 2 * slot] * rows, rows)
        attend_block(sizes, head_of(q_ref), kv_ref, bias, (acc_ref, max_ref, sum_ref), OWN, False, finish)

    @pl.when(use == NONE)
    def _():
        finish(slice(0, kv_heads))

    for g in range(kv_heads):
        store(g).wait()


def calls(sizes, n_docs, info, mated):
    kv_heads, group_size, rows = sizes
    tall = group_size * rows
    sets = 2 if mated else 1
    state = [
        pltpu.VMEM((sets, kv_heads, HD, tall), jnp.float32),
        pltpu.VMEM((sets, kv_heads, tall), jnp.float32),
        pltpu.VMEM((sets, kv_heads, tall), jnp.float32),
    ]
    smem, vmem = pl.BlockSpec(memory_space=pltpu.SMEM), pl.BlockSpec(memory_space=pltpu.VMEM)
    held = []

    def call(kernel, arrays, out, name, keeps=True, flops=FLOPS):
        n_in = 1 + len(arrays)
        out = out + (state if keeps else [])
        result = pl.pallas_call(
            kernel,
            out_shape=out,
            in_specs=[smem] + [vmem] * (len(arrays) + len(held)),
            out_specs=[vmem] * len(out),
            input_output_aliases={n_in + k: len(out) - 3 + k for k in range(len(held))} if keeps else {},
            compiler_params=pltpu.CompilerParams(vmem_limit_bytes=VMEM_LIMIT),
            cost_estimate=pl.CostEstimate(flops=flops, bytes_accessed=1024, transcendentals=0),
            name=name,
        )(info, *arrays, *held)
        if not keeps:
            return result
        held[:] = result[-3:]
        return result[:-3]

    def own(q, kv):
        call(functools.partial(own_kernel, sizes, n_docs), [q, kv], [], "own_block")

    def add(slot, q, qm, kv):
        qs = [q] if qm is None else [q, qm]
        kernel = functools.partial(add_kernel, sizes, n_docs, slot, qm is not None)
        call(kernel, qs + [kv], [], "add_block")

    def part(slot, q, qm, kv):
        out = jax.ShapeDtypeStruct((rows, (kv_heads + 1) * group_size * HD), jnp.bfloat16)
        return call(functools.partial(part_kernel, sizes, n_docs, slot), [q, qm, kv], [out], "mate_part")[0]

    def touch(kv):
        call(touch_kernel, [kv], [], "last_block_here", flops=LAST_FLOPS)

    def last(slot, q, parts, kv):
        return pl.pallas_call(
            functools.partial(last_kernel, sizes, n_docs, slot, mated),
            out_shape=jax.ShapeDtypeStruct((rows, kv_heads * group_size * HD), jnp.bfloat16),
            in_specs=[smem] + [vmem] * (2 + len(parts) + len(held)),
            out_specs=pl.BlockSpec(memory_space=pltpu.HBM),
            scratch_shapes=[
                pltpu.VMEM((rows, kv_heads * group_size * HD), jnp.bfloat16),
                pltpu.SemaphoreType.DMA((kv_heads,)),
            ],
            compiler_params=pltpu.CompilerParams(vmem_limit_bytes=VMEM_LIMIT),
            name="last_block",
        )(info, q, *parts, kv, *held)

    def after(block):
        block, held[-1] = lax.optimization_barrier((block, held[-1]))
        return block

    return own, add, part, touch, last, after


def pack(keys, values, lengths, pack_order, table):
    rows, width = keys.shape
    n_docs = lengths.shape[0]
    hbm = pl.BlockSpec(memory_space=pltpu.HBM)
    scalars = [lengths, pack_order] + ([] if table is None else [table])
    return pl.pallas_call(
        functools.partial(pack_kernel, rows, n_docs, table is not None),
        out_shape=[
            pltpu.VMEM((rows, 2 * width), keys.dtype),
            pltpu.SMEM((STARTS + n_docs,), jnp.int32),
        ],
        in_specs=[hbm] * (len(scalars) + 2),
        out_specs=[pl.BlockSpec(memory_space=pltpu.VMEM), pl.BlockSpec(memory_space=pltpu.SMEM)],
        scratch_shapes=[
            pltpu.VMEM((rows, width), values.dtype),
            pltpu.SMEM((n_docs,), jnp.int32),
            pltpu.SMEM((n_docs,), jnp.int32),
            pltpu.SMEM((1 + 2 * SLOTS,), jnp.int32),
            pltpu.SemaphoreType.DMA((5,)),
        ],
        name="pack_keys_values",
    )(*scalars, keys, values)


def ring_shards(groups, queries, keys, values, lengths, pack_order):
    rows, kv_heads = queries.shape[0], keys.shape[1] // HD
    m = len(RING)
    sizes = (kv_heads, queries.shape[1] // keys.shape[1], rows)
    route, user, straight = make_plan(groups, FIRST // rows)
    table = jnp.array(block_table(route, user, straight, groups), jnp.int32)
    kv, info = pack(keys, values, lengths, pack_order, table)
    own, add, part, touch, last, after = calls(sizes, lengths.shape[0], info, True)

    def send(block, op, step):
        return lax.ppermute(block, AXES, sorted((e, d) for d, (e, _) in route[op, step].items()))

    mates = [(d, d ^ m) for d in range(groups * m)]
    eight_back = [(d - m, d) for o in range(2, groups, 2) for d in range(o * m, (o + 1) * m)]
    busy = [(e, d) for e, d in eight_back if d % m in (3, 4)]
    u1 = send(kv, "own", 1)
    kvm = lax.ppermute(kv, AXES, mates)
    q = fetched(queries)
    own(q, kv)
    w1 = send(after(kvm), "mate", 1)
    qm = lax.ppermute(queries, AXES, mates)
    beside = [[(e, q)] for _, q, e in straight]
    near = [lax.ppermute(kv, AXES, beside[0] + busy)]
    u2 = send(after(u1), "own", 2)
    add(7, q, None, kvm)
    add(0, q, qm, u1)
    w2 = send(after(w1), "mate", 2)
    add(1, q, qm, w1)
    add(9, q, None, near[0])
    near += [lax.ppermute(after(w1), AXES, beside[1]), lax.ppermute(u1, AXES, beside[2])]
    kv8 = lax.ppermute(after(kv), AXES, [x for x in eight_back if x not in busy])
    u3 = send(after(u2), "own", 3)
    add(2, q, qm, u2)
    w3 = send(after(w2), "mate", 3)
    add(3, q, qm, w2)
    u4 = send(after(u3), "own", 4)
    add(4, q, qm, u3)
    add(10, q, None, near[1])
    add(11, q, None, near[2])
    mine = part(5, q, qm, w3)
    theirs = lax.ppermute(mine, AXES, mates)
    add(8, q, None, kv8)
    touch(u4)
    return last(6, q, [theirs], u4)


def chain_shards(queries, keys, values, lengths, pack_order):
    rows, kv_heads = queries.shape[0], keys.shape[1] // HD
    sizes = (kv_heads, queries.shape[1] // keys.shape[1], rows)
    n = lax.axis_size(AXES)
    kv, info = pack(keys, values, lengths, pack_order, None)
    own, add, part, touch, last, after = calls(sizes, lengths.shape[0], info, False)
    q = queries
    own(q, kv)
    for hop in range(HOPS):
        kv = lax.ppermute(kv, AXES, [(d, d + 1) for d in range(n - 1)])
        if hop < HOPS - 1:
            add(hop, q, None, kv)
    return last(HOPS - 1, q, [], kv)


def solution(mesh):
    spec, whole = P(AXES, None), P()
    outer, inner = mesh.shape["outer"], mesh.shape["inner"]
    ring = outer == 4 and inner == len(RING) == HOPS
    shards = functools.partial(ring_shards, outer) if ring else chain_shards
    return jax.shard_map(
        shards, mesh=mesh, in_specs=(spec, spec, spec, whole, whole), out_specs=spec, check_vma=False
    )
```

```python
import functools
import math

import jax
import jax.numpy as jnp
from jax import lax
from jax.experimental import pallas as pl
from jax.experimental.pallas import tpu as pltpu
from jax.sharding import PartitionSpec as P

HD = 128
HOPS = 8
FIRST = 1024
AXES = ("outer", "inner")
NEG = -1e30
SCALE = math.log2(math.e) / math.sqrt(HD)
RING = (0, 2, 4, 6, 7, 5, 3, 1)
OWN, MATE, NONE = 0, 1, 2
VMEM_LIMIT = 40 * 1024 * 1024
SLOTS = 12
STARTS = 2 + 2 * SLOTS
FLOPS = 1000
LAST_FLOPS = 50_000_000_000


def make_plan(groups, first_blocks):
    m = len(RING)
    n = groups * m
    place = {j: p for p, j in enumerate(RING)}

    def held(chip, odd, j):
        x, i = divmod(chip, m)
        o = 2 * x + odd
        if odd and j > i and (i, j) != (0, 1):
            o = (o + 2) % groups
        return o * m + j

    last = n - m
    straight = [
        (last + 2, last + 3, last + 2),
        (last + 3, last + 4, last - m + 5),
        (last - 2 * m + 1, last - m, last - 2 * m),
    ]

    def uses(q, b):
        return 0 < q - b <= HOPS and not (b < first_blocks <= q) and (b, q) not in [x[:2] for x in straight]

    def user(d, b):
        return d if uses(d, b) else d ^ m if uses(d ^ m, b) else None

    ops = [("own", 1), ("mate", 1), ("own", 2), ("mate", 2), ("own", 3), ("mate", 3), ("own", 4)]
    route = {}
    for op, s in ops:
        route[op, s] = {}
        for d in range(n):
            o, i = divmod(d, m)
            x, core = divmod(o, 2)
            odd = core if op == "own" else 1 - core
            way = 1 if core else -1
            j = RING[(place[i] - way * s) % m]
            b = held(x * m + i, odd, j)
            behind = RING[(place[i] - way) % m]
            (source,) = [
                (2 * y + core) * m + behind for y in range(groups // 2) if held(y * m + behind, odd, j) == b
            ]
            route[op, s][d] = (source, b)
    for op, s in reversed(ops):
        sends_on = {e for e, _ in route.get((op, s + 1), {}).values()}
        route[op, s] = {d: r for d, r in route[op, s].items() if user(d, r[1]) is not None or d in sends_on}
    route["own", 4] = {user(d, b): (e, b) for d, (e, b) in route["own", 4].items()}
    return route, user, straight


def block_table(route, user, straight, groups):
    m = len(RING)
    rows = []
    for d in range(groups * m):
        row = [d ^ m]
        for key in [("own", 1), ("mate", 1), ("own", 2), ("mate", 2), ("own", 3), ("mate", 3), ("own", 4)]:
            if d not in route[key]:
                row += [0, NONE]
                continue
            b = route[key][d][1]
            u = d if key == ("own", 4) else user(d, b)
            row += [b, NONE if u is None else OWN if u == d else MATE]
        row += [d ^ m, OWN if user(d, d ^ m) == d else NONE]
        o = d // m
        back = [d - m, OWN] if o % 2 == 0 and o > 0 else [0, NONE]
        early = d % m in (3, 4)
        row += [0, NONE] if early else back
        for b, q, e in straight:
            row += [b, OWN] if q == d else back if early and b == e else [0, NONE]
        rows.append(row)
    return rows


def position(axes):
    outer, inner = axes
    return lax.axis_index(outer) * lax.axis_size(inner) + lax.axis_index(inner)


def attend_block(sizes, q_of, kv_ref, bias, state, u, fresh, finish=None):
    kv_heads, group_size, _ = sizes
    acc_ref, max_ref, sum_ref = state
    tile = 2 if group_size % 2 == 0 else 1
    bias = jnp.concatenate([bias] * tile, axis=1)
    for g in range(kv_heads):
        row = slice(g, g + 1)
        keys = kv_ref[:, g * HD : (g + 1) * HD]
        values = kv_ref[:, (kv_heads + g) * HD : (kv_heads + g + 1) * HD]
        for j in range(0, group_size, tile):
            columns = slice(j * HD, (j + tile) * HD)
            queries = jnp.concatenate([q_of(g * group_size + j + k) for k in range(tile)], axis=0)
            s = lax.dot_general(keys, queries, (((1,), (1,)), ((), ())), preferred_element_type=jnp.float32)
            s = s * SCALE + bias
            top = jnp.max(s, axis=0, keepdims=True)
            if not fresh:
                old = max_ref[u, row, columns]
                top = jnp.maximum(old, top)
                fade = jnp.exp2(old - top)
            p = jnp.exp2(s - top)
            total = jnp.sum(p, axis=0, keepdims=True)
            mixed = jnp.dot(values, p.astype(jnp.bfloat16), preferred_element_type=jnp.float32)
            max_ref[u, row, columns] = top
            sum_ref[u, row, columns] = total if fresh else sum_ref[u, row, columns] * fade + total
            acc_ref[u, g, :, columns] = mixed if fresh else acc_ref[u, g, :, columns] * fade + mixed
        if finish is not None and (g + 1) % (kv_heads // 2) == 0:
            finish(slice(g + 1 - kv_heads // 2, g + 1))


def head_of(ref):
    return lambda h: ref[:, h * HD : (h + 1) * HD]


def mask_bias(info_ref, n_docs, query_base, key_base, rows):
    query_pos = query_base + lax.broadcasted_iota(jnp.int32, (8, rows), 1)

    def latest(j, seen):
        start = info_ref[STARTS + j]
        return jnp.where(start <= query_pos, start, seen)

    seen = lax.fori_loop(0, n_docs, latest, jnp.zeros((8, rows), jnp.int32), unroll=n_docs <= 8)
    seen, query_pos = (jnp.concatenate([x] * (rows // 8), axis=0) for x in (seen, query_pos))
    key_pos = key_base + lax.broadcasted_iota(jnp.int32, (rows, rows), 0)
    return jnp.where((key_pos >= seen) & (key_pos <= query_pos), 0.0, NEG).astype(jnp.float32)


def pack_kernel(rows, n_docs, table, *refs):
    *far, k_ref, v_ref, kv_ref, info_ref, v_here, lengths_ref, order_ref, row_ref, sems = refs
    width = k_ref.shape[1]
    device = position(AXES)
    fetch_v = pltpu.make_async_copy(v_ref, v_here, sems.at[0])
    fetch_k = pltpu.make_async_copy(k_ref, kv_ref.at[:, pl.ds(0, width)], sems.at[1])
    small = [(far[0], lengths_ref), (far[1], order_ref)] + ([(far[2].at[device], row_ref)] if table else [])
    fetches = [pltpu.make_async_copy(a, b, sems.at[2 + k]) for k, (a, b) in enumerate(small)]
    for fetch in [fetch_v, fetch_k, *fetches]:
        fetch.start()
    for fetch in fetches:
        fetch.wait()

    mate = row_ref[0] if table else device
    info_ref[0] = device
    info_ref[1] = mate
    own_first, mate_first = device * rows, mate * rows

    def document(j, carry):
        start, own_seen, mate_seen = carry
        info_ref[STARTS + j] = start
        own_seen = jnp.where(start <= own_first, start, own_seen)
        mate_seen = jnp.where(start <= mate_first, start, mate_seen)
        return start + lengths_ref[order_ref[j]], own_seen, mate_seen

    zero = jnp.int32(0)
    _, own_seen, mate_seen = lax.fori_loop(0, n_docs, document, (zero, zero, zero), unroll=n_docs <= 8)
    for slot in range(SLOTS):
        if table:
            block, use = row_ref[1 + 2 * slot], row_ref[2 + 2 * slot]
        else:
            block, use = device - 1 - slot, OWN
        seen = jnp.where(use == OWN, own_seen, mate_seen)
        shown = (block >= 0) & (block * rows + rows > seen)
        info_ref[2 + 2 * slot] = block
        info_ref[3 + 2 * slot] = jnp.where(shown, use, NONE)

    fetch_v.wait()
    for g in range(width // HD):
        kv_ref[:, width + g * HD : width + (g + 1) * HD] = v_here[:, g * HD : (g + 1) * HD].T
    fetch_k.wait()


def fetch_kernel(q_ref, here_ref, sem):
    fetch = pltpu.make_async_copy(q_ref, here_ref, sem)
    fetch.start()
    fetch.wait()


def fetched(queries):
    return pl.pallas_call(
        fetch_kernel,
        out_shape=pltpu.VMEM(queries.shape, queries.dtype),
        in_specs=[pl.BlockSpec(memory_space=pltpu.HBM)],
        out_specs=pl.BlockSpec(memory_space=pltpu.VMEM),
        scratch_shapes=[pltpu.SemaphoreType.DMA],
        name="fetch_queries",
    )(queries)


def own_kernel(sizes, n_docs, info_ref, q_ref, kv_ref, *state):
    rows = sizes[2]
    base = info_ref[0] * rows
    bias = mask_bias(info_ref, n_docs, base, base, rows)
    attend_block(sizes, head_of(q_ref), kv_ref, bias, state, OWN, True)


def add_block(sizes, n_docs, slot, info_ref, q_ref, qm_ref, kv_ref, state):
    rows = sizes[2]
    use = info_ref[3 + 2 * slot]

    @pl.when(use != NONE)
    def _():
        mine = use == OWN
        query_base = jnp.where(mine, info_ref[0], info_ref[1]) * rows
        bias = mask_bias(info_ref, n_docs, query_base, info_ref[2 + 2 * slot] * rows, rows)
        q_of = head_of(q_ref)
        if qm_ref is not None:
            q_own, q_mate = q_of, head_of(qm_ref)
            q_of = lambda h: jnp.where(mine, q_own(h), q_mate(h))
        attend_block(sizes, q_of, kv_ref, bias, state, use, False)


def add_kernel(sizes, n_docs, slot, mated, clear, info_ref, q_ref, *refs):
    qm_ref, refs = (refs[0], refs[1:]) if mated else (None, refs)
    if clear:
        for ref, value in zip(refs[4:], (0.0, NEG, 0.0)):
            ref[MATE] = jnp.full(ref.shape[1:], value, jnp.float32)
    add_block(sizes, n_docs, slot, info_ref, q_ref, qm_ref, refs[0], refs[4:])


def split3(x):
    a = x.astype(jnp.bfloat16)
    rest = x - a.astype(jnp.float32)
    b = rest.astype(jnp.bfloat16)
    return a, b, (rest - b.astype(jnp.float32)).astype(jnp.bfloat16)


def part_kernel(sizes, n_docs, slot, info_ref, q_ref, qm_ref, kv_ref, a_in, m_in, s_in, part_ref, *state):
    kv_heads, group_size, rows = sizes
    add_block(sizes, n_docs, slot, info_ref, q_ref, qm_ref, kv_ref, state)
    acc_ref, max_ref, sum_ref = state
    width = group_size * HD
    totals = sum_ref[MATE]
    shares = 1.0 / jnp.where(totals > 0, totals, 1.0)
    for g in range(kv_heads):
        part_ref[:, g * width : (g + 1) * width] = (acc_ref[MATE, g] * shares[g : g + 1]).astype(jnp.bfloat16)
    stats = jnp.concatenate([max_ref[MATE], totals], axis=0)
    for k, piece in enumerate(split3(stats)):
        part_ref[2 * k * kv_heads : 2 * (k + 1) * kv_heads, kv_heads * width :] = piece


def touch_kernel(info_ref, kv_ref, *refs):
    pass


def last_kernel(sizes, n_docs, slot, mated, info_ref, q_ref, *refs):
    kv_heads, group_size, rows = sizes
    width = group_size * HD
    part_ref, refs = (refs[0], refs[1:]) if mated else (None, refs)
    kv_ref, acc_ref, max_ref, sum_ref, out_ref, out_here, sems = refs
    if mated:
        stats = sum(
            part_ref[2 * k * kv_heads : 2 * (k + 1) * kv_heads, kv_heads * width :].astype(jnp.float32) for k in range(3)
        )
        tops, sums = stats[:kv_heads], stats[kv_heads:]

    def store(g):
        columns = pl.ds(g * width, width)
        return pltpu.make_async_copy(out_here.at[:, columns], out_ref.at[:, columns], sems.at[g])

    def finish(some):
        top, total = max_ref[OWN, some], sum_ref[OWN, some]
        if mated:
            both = jnp.maximum(top, tops[some])
            weight, other = jnp.exp2(top - both), jnp.exp2(tops[some] - both) * sums[some]
            share = 1.0 / (total * weight + other)
            mine, others = weight * share, other * share
        else:
            mine = 1.0 / total
        for k, g in enumerate(range(some.start, some.stop)):
            out = acc_ref[OWN, g] * mine[k : k + 1]
            if mated:
                theirs = part_ref[:, g * width : (g + 1) * width].astype(jnp.float32)
                out = out + theirs * others[k : k + 1]
            out = out.astype(jnp.bfloat16)
            for j in range(group_size):
                h = g * group_size + j
                out_here[:, h * HD : (h + 1) * HD] = out[:, j * HD : (j + 1) * HD].T
            store(g).start()

    use = info_ref[3 + 2 * slot]

    @pl.when(use != NONE)
    def _():
        bias = mask_bias(info_ref, n_docs, info_ref[0] * rows, info_ref[2 + 2 * slot] * rows, rows)
        attend_block(sizes, head_of(q_ref), kv_ref, bias, (acc_ref, max_ref, sum_ref), OWN, False, finish)

    @pl.when(use == NONE)
    def _():
        finish(slice(0, kv_heads))

    for g in range(kv_heads):
        store(g).wait()


def calls(sizes, n_docs, info, mated):
    kv_heads, group_size, rows = sizes
    tall = group_size * rows
    sets = 2 if mated else 1
    state = [
        pltpu.VMEM((sets, kv_heads, HD, tall), jnp.float32),
        pltpu.VMEM((sets, kv_heads, tall), jnp.float32),
        pltpu.VMEM((sets, kv_heads, tall), jnp.float32),
    ]
    smem, vmem = pl.BlockSpec(memory_space=pltpu.SMEM), pl.BlockSpec(memory_space=pltpu.VMEM)
    held = []

    def call(kernel, arrays, out, name, keeps=True, flops=FLOPS):
        n_in = 1 + len(arrays)
        out = out + (state if keeps else [])
        result = pl.pallas_call(
            kernel,
            out_shape=out,
            in_specs=[smem] + [vmem] * (len(arrays) + len(held)),
            out_specs=[vmem] * len(out),
            input_output_aliases={n_in + k: len(out) - 3 + k for k in range(len(held))} if keeps else {},
            compiler_params=pltpu.CompilerParams(vmem_limit_bytes=VMEM_LIMIT),
            cost_estimate=pl.CostEstimate(flops=flops, bytes_accessed=1024, transcendentals=0),
            name=name,
        )(info, *arrays, *held)
        if not keeps:
            return result
        held[:] = result[-3:]
        return result[:-3]

    def own(q, kv):
        call(functools.partial(own_kernel, sizes, n_docs), [q, kv], [], "own_block")

    def add(slot, q, qm, kv, clear=False):
        qs = [q] if qm is None else [q, qm]
        kernel = functools.partial(add_kernel, sizes, n_docs, slot, qm is not None, clear)
        call(kernel, qs + [kv], [], "add_block")

    def part(slot, q, qm, kv):
        out = jax.ShapeDtypeStruct((rows, (kv_heads + 1) * group_size * HD), jnp.bfloat16)
        return call(functools.partial(part_kernel, sizes, n_docs, slot), [q, qm, kv], [out], "mate_part")[0]

    def touch(kv):
        call(touch_kernel, [kv], [], "last_block_here", flops=LAST_FLOPS)

    def last(slot, q, parts, kv):
        return pl.pallas_call(
            functools.partial(last_kernel, sizes, n_docs, slot, mated),
            out_shape=jax.ShapeDtypeStruct((rows, kv_heads * group_size * HD), jnp.bfloat16),
            in_specs=[smem] + [vmem] * (2 + len(parts) + len(held)),
            out_specs=pl.BlockSpec(memory_space=pltpu.HBM),
            scratch_shapes=[
                pltpu.VMEM((rows, kv_heads * group_size * HD), jnp.bfloat16),
                pltpu.SemaphoreType.DMA((kv_heads,)),
            ],
            compiler_params=pltpu.CompilerParams(vmem_limit_bytes=VMEM_LIMIT),
            name="last_block",
        )(info, q, *parts, kv, *held)

    def after(block):
        block, held[-1] = lax.optimization_barrier((block, held[-1]))
        return block

    return own, add, part, touch, last, after


def pack(keys, values, lengths, pack_order, table):
    rows, width = keys.shape
    n_docs = lengths.shape[0]
    hbm = pl.BlockSpec(memory_space=pltpu.HBM)
    scalars = [lengths, pack_order] + ([] if table is None else [table])
    return pl.pallas_call(
        functools.partial(pack_kernel, rows, n_docs, table is not None),
        out_shape=[
            pltpu.VMEM((rows, 2 * width), keys.dtype),
            pltpu.SMEM((STARTS + n_docs,), jnp.int32),
        ],
        in_specs=[hbm] * (len(scalars) + 2),
        out_specs=[pl.BlockSpec(memory_space=pltpu.VMEM), pl.BlockSpec(memory_space=pltpu.SMEM)],
        scratch_shapes=[
            pltpu.VMEM((rows, width), values.dtype),
            pltpu.SMEM((n_docs,), jnp.int32),
            pltpu.SMEM((n_docs,), jnp.int32),
            pltpu.SMEM((1 + 2 * SLOTS,), jnp.int32),
            pltpu.SemaphoreType.DMA((5,)),
        ],
        name="pack_keys_values",
    )(*scalars, keys, values)


def ring_shards(groups, queries, keys, values, lengths, pack_order):
    rows, kv_heads = queries.shape[0], keys.shape[1] // HD
    m = len(RING)
    sizes = (kv_heads, queries.shape[1] // keys.shape[1], rows)
    route, user, straight = make_plan(groups, FIRST // rows)
    table = jnp.array(block_table(route, user, straight, groups), jnp.int32)
    kv, info = pack(keys, values, lengths, pack_order, table)
    own, add, part, touch, last, after = calls(sizes, lengths.shape[0], info, True)

    def send(block, op, step):
        return lax.ppermute(block, AXES, sorted((e, d) for d, (e, _) in route[op, step].items()))

    mates = [(d, d ^ m) for d in range(groups * m)]
    eight_back = [(d - m, d) for o in range(2, groups, 2) for d in range(o * m, (o + 1) * m)]
    busy = [(e, d) for e, d in eight_back if d % m in (3, 4)]
    u1 = send(kv, "own", 1)
    kvm = lax.ppermute(kv, AXES, mates)
    q = fetched(queries)
    own(q, kv)
    w1 = send(after(kvm), "mate", 1)
    qm = lax.ppermute(queries, AXES, mates)
    beside = [[(e, q)] for _, q, e in straight]
    near = [lax.ppermute(kv, AXES, beside[0] + busy)]
    u2 = send(after(u1), "own", 2)
    add(7, q, None, kvm, clear=True)
    add(0, q, qm, u1)
    w2 = send(after(w1), "mate", 2)
    add(1, q, qm, w1)
    add(9, q, None, near[0])
    near += [lax.ppermute(after(w1), AXES, beside[1]), lax.ppermute(u1, AXES, beside[2])]
    kv8 = lax.ppermute(after(kv), AXES, [x for x in eight_back if x not in busy])
    u3 = send(after(u2), "own", 3)
    add(2, q, qm, u2)
    w3 = send(after(w2), "mate", 3)
    add(3, q, qm, w2)
    u4 = send(after(u3), "own", 4)
    add(4, q, qm, u3)
    add(11, q, None, near[2])
    mine = part(5, q, qm, w3)
    theirs = lax.ppermute(mine, AXES, mates)
    add(8, q, None, kv8)
    add(10, q, None, near[1])
    touch(u4)
    return last(6, q, [theirs], u4)


def chain_shards(queries, keys, values, lengths, pack_order):
    rows, kv_heads = queries.shape[0], keys.shape[1] // HD
    sizes = (kv_heads, queries.shape[1] // keys.shape[1], rows)
    n = lax.axis_size(AXES)
    kv, info = pack(keys, values, lengths, pack_order, None)
    own, add, part, touch, last, after = calls(sizes, lengths.shape[0], info, False)
    q = queries
    own(q, kv)
    for hop in range(HOPS):
        kv = lax.ppermute(kv, AXES, [(d, d + 1) for d in range(n - 1)])
        if hop < HOPS - 1:
            add(hop, q, None, kv)
    return last(HOPS - 1, q, [], kv)


def solution(mesh):
    spec, whole = P(AXES, None), P()
    outer, inner = mesh.shape["outer"], mesh.shape["inner"]
    ring = outer == 4 and inner == len(RING) == HOPS
    shards = functools.partial(ring_shards, outer) if ring else chain_shards
    return jax.shard_map(
        shards, mesh=mesh, in_specs=(spec, spec, spec, whole, whole), out_specs=spec, check_vma=False
    )
```

```python
import functools
import math

import jax
import jax.numpy as jnp
from jax import lax
from jax.experimental import pallas as pl
from jax.experimental.pallas import tpu as pltpu
from jax.sharding import PartitionSpec as P

HD = 128
HOPS = 8
FIRST = 1024
AXES = ("outer", "inner")
NEG = -1e30
SCALE = math.log2(math.e) / math.sqrt(HD)
RING = (0, 2, 4, 6, 7, 5, 3, 1)
OWN, MATE, NONE = 0, 1, 2
VMEM_LIMIT = 40 * 1024 * 1024
SLOTS = 12
STARTS = 2 + 2 * SLOTS
FLOPS = 1000
LAST_FLOPS = 50_000_000_000


def make_plan(groups, first_blocks):
    m = len(RING)
    n = groups * m
    place = {j: p for p, j in enumerate(RING)}

    def held(chip, odd, j):
        x, i = divmod(chip, m)
        o = 2 * x + odd
        if odd and j > i and (i, j) != (0, 1):
            o = (o + 2) % groups
        return o * m + j

    last = n - m
    straight = [
        (last + 2, last + 3, last + 2),
        (last + 3, last + 4, last - m + 5),
        (last - 2 * m + 1, last - m, last - 2 * m),
    ]

    def uses(q, b):
        return 0 < q - b <= HOPS and not (b < first_blocks <= q) and (b, q) not in [x[:2] for x in straight]

    def user(d, b):
        return d if uses(d, b) else d ^ m if uses(d ^ m, b) else None

    ops = [("own", 1), ("mate", 1), ("own", 2), ("mate", 2), ("own", 3), ("mate", 3), ("own", 4)]
    route = {}
    for op, s in ops:
        route[op, s] = {}
        for d in range(n):
            o, i = divmod(d, m)
            x, core = divmod(o, 2)
            odd = core if op == "own" else 1 - core
            way = 1 if core else -1
            j = RING[(place[i] - way * s) % m]
            b = held(x * m + i, odd, j)
            behind = RING[(place[i] - way) % m]
            (source,) = [
                (2 * y + core) * m + behind for y in range(groups // 2) if held(y * m + behind, odd, j) == b
            ]
            route[op, s][d] = (source, b)
    for op, s in reversed(ops):
        sends_on = {e for e, _ in route.get((op, s + 1), {}).values()}
        route[op, s] = {d: r for d, r in route[op, s].items() if user(d, r[1]) is not None or d in sends_on}
    route["own", 4] = {user(d, b): (e, b) for d, (e, b) in route["own", 4].items()}
    return route, user, straight


def block_table(route, user, straight, groups):
    m = len(RING)
    rows = []
    for d in range(groups * m):
        row = [d ^ m]
        for key in [("own", 1), ("mate", 1), ("own", 2), ("mate", 2), ("own", 3), ("mate", 3), ("own", 4)]:
            if d not in route[key]:
                row += [0, NONE]
                continue
            b = route[key][d][1]
            u = d if key == ("own", 4) else user(d, b)
            row += [b, NONE if u is None else OWN if u == d else MATE]
        row += [d ^ m, OWN if user(d, d ^ m) == d else NONE]
        o = d // m
        back = [d - m, OWN] if o % 2 == 0 and o > 0 else [0, NONE]
        early = d % m in (3, 4)
        row += [0, NONE] if early else back
        for b, q, e in straight:
            row += [b, OWN] if q == d else back if early and b == e else [0, NONE]
        rows.append(row)
    return rows


def position(axes):
    outer, inner = axes
    return lax.axis_index(outer) * lax.axis_size(inner) + lax.axis_index(inner)


def attend_block(sizes, q_of, kv_ref, bias, state, u, fresh, finish=None):
    kv_heads, group_size, _ = sizes
    acc_ref, max_ref, sum_ref = state
    tile = 2 if group_size % 2 == 0 else 1
    bias = jnp.concatenate([bias] * tile, axis=1)
    for g in range(kv_heads):
        row = slice(g, g + 1)
        keys = kv_ref[:, g * HD : (g + 1) * HD]
        values = kv_ref[:, (kv_heads + g) * HD : (kv_heads + g + 1) * HD]
        for j in range(0, group_size, tile):
            columns = slice(j * HD, (j + tile) * HD)
            queries = jnp.concatenate([q_of(g * group_size + j + k) for k in range(tile)], axis=0)
            s = lax.dot_general(keys, queries, (((1,), (1,)), ((), ())), preferred_element_type=jnp.float32)
            s = s * SCALE + bias
            top = jnp.max(s, axis=0, keepdims=True)
            if not fresh:
                old = max_ref[u, row, columns]
                top = jnp.maximum(old, top)
                fade = jnp.exp2(old - top)
            p = jnp.exp2(s - top)
            total = jnp.sum(p, axis=0, keepdims=True)
            mixed = jnp.dot(values, p.astype(jnp.bfloat16), preferred_element_type=jnp.float32)
            max_ref[u, row, columns] = top
            sum_ref[u, row, columns] = total if fresh else sum_ref[u, row, columns] * fade + total
            acc_ref[u, g, :, columns] = mixed if fresh else acc_ref[u, g, :, columns] * fade + mixed
        if finish is not None and (g + 1) % (kv_heads // 2) == 0:
            finish(slice(g + 1 - kv_heads // 2, g + 1))


def head_of(ref):
    return lambda h: ref[:, h * HD : (h + 1) * HD]


def mask_bias(info_ref, n_docs, query_base, key_base, rows):
    query_pos = query_base + lax.broadcasted_iota(jnp.int32, (8, rows), 1)

    def latest(j, seen):
        start = info_ref[STARTS + j]
        return jnp.where(start <= query_pos, start, seen)

    seen = lax.fori_loop(0, n_docs, latest, jnp.zeros((8, rows), jnp.int32), unroll=n_docs <= 8)
    seen, query_pos = (jnp.concatenate([x] * (rows // 8), axis=0) for x in (seen, query_pos))
    key_pos = key_base + lax.broadcasted_iota(jnp.int32, (rows, rows), 0)
    return jnp.where((key_pos >= seen) & (key_pos <= query_pos), 0.0, NEG).astype(jnp.float32)


def pack_kernel(rows, n_docs, table, *refs):
    *far, k_ref, v_ref, kv_ref, info_ref, v_here, lengths_ref, order_ref, row_ref, sems = refs
    width = k_ref.shape[1]
    device = position(AXES)
    fetch_v = pltpu.make_async_copy(v_ref, v_here, sems.at[0])
    fetch_k = pltpu.make_async_copy(k_ref, kv_ref.at[:, pl.ds(0, width)], sems.at[1])
    small = [(far[0], lengths_ref), (far[1], order_ref)] + ([(far[2].at[device], row_ref)] if table else [])
    fetches = [pltpu.make_async_copy(a, b, sems.at[2 + k]) for k, (a, b) in enumerate(small)]
    for fetch in [fetch_v, fetch_k, *fetches]:
        fetch.start()
    for fetch in fetches:
        fetch.wait()

    mate = row_ref[0] if table else device
    info_ref[0] = device
    info_ref[1] = mate
    own_first, mate_first = device * rows, mate * rows

    def document(j, carry):
        start, own_seen, mate_seen = carry
        info_ref[STARTS + j] = start
        own_seen = jnp.where(start <= own_first, start, own_seen)
        mate_seen = jnp.where(start <= mate_first, start, mate_seen)
        return start + lengths_ref[order_ref[j]], own_seen, mate_seen

    zero = jnp.int32(0)
    _, own_seen, mate_seen = lax.fori_loop(0, n_docs, document, (zero, zero, zero), unroll=n_docs <= 8)
    for slot in range(SLOTS):
        if table:
            block, use = row_ref[1 + 2 * slot], row_ref[2 + 2 * slot]
        else:
            block, use = device - 1 - slot, OWN
        seen = jnp.where(use == OWN, own_seen, mate_seen)
        shown = (block >= 0) & (block * rows + rows > seen)
        info_ref[2 + 2 * slot] = block
        info_ref[3 + 2 * slot] = jnp.where(shown, use, NONE)

    fetch_v.wait()
    for g in range(width // HD):
        kv_ref[:, width + g * HD : width + (g + 1) * HD] = v_here[:, g * HD : (g + 1) * HD].T
    fetch_k.wait()


def fetch_kernel(q_ref, here_ref, sem):
    fetch = pltpu.make_async_copy(q_ref, here_ref, sem)
    fetch.start()
    fetch.wait()


def fetched(queries):
    return pl.pallas_call(
        fetch_kernel,
        out_shape=pltpu.VMEM(queries.shape, queries.dtype),
        in_specs=[pl.BlockSpec(memory_space=pltpu.HBM)],
        out_specs=pl.BlockSpec(memory_space=pltpu.VMEM),
        scratch_shapes=[pltpu.SemaphoreType.DMA],
        name="fetch_queries",
    )(queries)


def own_kernel(sizes, n_docs, info_ref, q_ref, kv_ref, *state):
    rows = sizes[2]
    base = info_ref[0] * rows
    bias = mask_bias(info_ref, n_docs, base, base, rows)
    attend_block(sizes, head_of(q_ref), kv_ref, bias, state, OWN, True)
    if state[0].shape[0] > 1:
        for ref, value in zip(state, (0.0, NEG, 0.0)):
            ref[MATE] = jnp.full(ref.shape[1:], value, jnp.float32)


def add_block(sizes, n_docs, slot, info_ref, q_ref, qm_ref, kv_ref, state):
    rows = sizes[2]
    use = info_ref[3 + 2 * slot]

    @pl.when(use != NONE)
    def _():
        mine = use == OWN
        query_base = jnp.where(mine, info_ref[0], info_ref[1]) * rows
        bias = mask_bias(info_ref, n_docs, query_base, info_ref[2 + 2 * slot] * rows, rows)
        q_of = head_of(q_ref)
        if qm_ref is not None:
            q_own, q_mate = q_of, head_of(qm_ref)
            q_of = lambda h: jnp.where(mine, q_own(h), q_mate(h))
        attend_block(sizes, q_of, kv_ref, bias, state, use, False)


def add_kernel(sizes, n_docs, slot, mated, info_ref, q_ref, *refs):
    qm_ref, refs = (refs[0], refs[1:]) if mated else (None, refs)
    add_block(sizes, n_docs, slot, info_ref, q_ref, qm_ref, refs[0], refs[4:])


def split3(x):
    a = x.astype(jnp.bfloat16)
    rest = x - a.astype(jnp.float32)
    b = rest.astype(jnp.bfloat16)
    return a, b, (rest - b.astype(jnp.float32)).astype(jnp.bfloat16)


def part_kernel(sizes, n_docs, slot, info_ref, q_ref, qm_ref, kv_ref, a_in, m_in, s_in, part_ref, *state):
    kv_heads, group_size, rows = sizes
    add_block(sizes, n_docs, slot, info_ref, q_ref, qm_ref, kv_ref, state)
    acc_ref, max_ref, sum_ref = state
    width = group_size * HD
    totals = sum_ref[MATE]
    shares = 1.0 / jnp.where(totals > 0, totals, 1.0)
    for g in range(kv_heads):
        part_ref[:, g * width : (g + 1) * width] = (acc_ref[MATE, g] * shares[g : g + 1]).astype(jnp.bfloat16)
    stats = jnp.concatenate([max_ref[MATE], totals], axis=0)
    for k, piece in enumerate(split3(stats)):
        part_ref[2 * k * kv_heads : 2 * (k + 1) * kv_heads, kv_heads * width :] = piece


def touch_kernel(info_ref, kv_ref, *refs):
    pass


def last_kernel(sizes, n_docs, slot, mated, info_ref, q_ref, *refs):
    kv_heads, group_size, rows = sizes
    width = group_size * HD
    part_ref, refs = (refs[0], refs[1:]) if mated else (None, refs)
    kv_ref, acc_ref, max_ref, sum_ref, out_ref, out_here, sems = refs
    if mated:
        stats = sum(
            part_ref[2 * k * kv_heads : 2 * (k + 1) * kv_heads, kv_heads * width :].astype(jnp.float32) for k in range(3)
        )
        tops, sums = stats[:kv_heads], stats[kv_heads:]

    def store(g):
        columns = pl.ds(g * width, width)
        return pltpu.make_async_copy(out_here.at[:, columns], out_ref.at[:, columns], sems.at[g])

    def finish(some):
        top, total = max_ref[OWN, some], sum_ref[OWN, some]
        if mated:
            both = jnp.maximum(top, tops[some])
            weight, other = jnp.exp2(top - both), jnp.exp2(tops[some] - both) * sums[some]
            share = 1.0 / (total * weight + other)
            mine, others = weight * share, other * share
        else:
            mine = 1.0 / total
        for k, g in enumerate(range(some.start, some.stop)):
            out = acc_ref[OWN, g] * mine[k : k + 1]
            if mated:
                theirs = part_ref[:, g * width : (g + 1) * width].astype(jnp.float32)
                out = out + theirs * others[k : k + 1]
            out = out.astype(jnp.bfloat16)
            for j in range(group_size):
                h = g * group_size + j
                out_here[:, h * HD : (h + 1) * HD] = out[:, j * HD : (j + 1) * HD].T
            store(g).start()

    use = info_ref[3 + 2 * slot]

    @pl.when(use != NONE)
    def _():
        bias = mask_bias(info_ref, n_docs, info_ref[0] * rows, info_ref[2 + 2 * slot] * rows, rows)
        attend_block(sizes, head_of(q_ref), kv_ref, bias, (acc_ref, max_ref, sum_ref), OWN, False, finish)

    @pl.when(use == NONE)
    def _():
        finish(slice(0, kv_heads))

    for g in range(kv_heads):
        store(g).wait()


def calls(sizes, n_docs, info, mated):
    kv_heads, group_size, rows = sizes
    tall = group_size * rows
    sets = 2 if mated else 1
    state = [
        pltpu.VMEM((sets, kv_heads, HD, tall), jnp.float32),
        pltpu.VMEM((sets, kv_heads, tall), jnp.float32),
        pltpu.VMEM((sets, kv_heads, tall), jnp.float32),
    ]
    smem, vmem = pl.BlockSpec(memory_space=pltpu.SMEM), pl.BlockSpec(memory_space=pltpu.VMEM)
    held = []

    def call(kernel, arrays, out, name, keeps=True, flops=FLOPS):
        n_in = 1 + len(arrays)
        out = out + (state if keeps else [])
        result = pl.pallas_call(
            kernel,
            out_shape=out,
            in_specs=[smem] + [vmem] * (len(arrays) + len(held)),
            out_specs=[vmem] * len(out),
            input_output_aliases={n_in + k: len(out) - 3 + k for k in range(len(held))} if keeps else {},
            compiler_params=pltpu.CompilerParams(vmem_limit_bytes=VMEM_LIMIT),
            cost_estimate=pl.CostEstimate(flops=flops, bytes_accessed=1024, transcendentals=0),
            name=name,
        )(info, *arrays, *held)
        if not keeps:
            return result
        held[:] = result[-3:]
        return result[:-3]

    def own(q, kv):
        call(functools.partial(own_kernel, sizes, n_docs), [q, kv], [], "own_block")

    def add(slot, q, qm, kv):
        qs = [q] if qm is None else [q, qm]
        kernel = functools.partial(add_kernel, sizes, n_docs, slot, qm is not None)
        call(kernel, qs + [kv], [], "add_block")

    def part(slot, q, qm, kv):
        out = jax.ShapeDtypeStruct((rows, (kv_heads + 1) * group_size * HD), jnp.bfloat16)
        return call(functools.partial(part_kernel, sizes, n_docs, slot), [q, qm, kv], [out], "mate_part")[0]

    def touch(kv):
        call(touch_kernel, [kv], [], "last_block_here", flops=LAST_FLOPS)

    def last(slot, q, parts, kv):
        return pl.pallas_call(
            functools.partial(last_kernel, sizes, n_docs, slot, mated),
            out_shape=jax.ShapeDtypeStruct((rows, kv_heads * group_size * HD), jnp.bfloat16),
            in_specs=[smem] + [vmem] * (2 + len(parts) + len(held)),
            out_specs=pl.BlockSpec(memory_space=pltpu.HBM),
            scratch_shapes=[
                pltpu.VMEM((rows, kv_heads * group_size * HD), jnp.bfloat16),
                pltpu.SemaphoreType.DMA((kv_heads,)),
            ],
            compiler_params=pltpu.CompilerParams(vmem_limit_bytes=VMEM_LIMIT),
            name="last_block",
        )(info, q, *parts, kv, *held)

    def after(block):
        block, held[-1] = lax.optimization_barrier((block, held[-1]))
        return block

    return own, add, part, touch, last, after


def pack(keys, values, lengths, pack_order, table):
    rows, width = keys.shape
    n_docs = lengths.shape[0]
    hbm = pl.BlockSpec(memory_space=pltpu.HBM)
    scalars = [lengths, pack_order] + ([] if table is None else [table])
    return pl.pallas_call(
        functools.partial(pack_kernel, rows, n_docs, table is not None),
        out_shape=[
            pltpu.VMEM((rows, 2 * width), keys.dtype),
            pltpu.SMEM((STARTS + n_docs,), jnp.int32),
        ],
        in_specs=[hbm] * (len(scalars) + 2),
        out_specs=[pl.BlockSpec(memory_space=pltpu.VMEM), pl.BlockSpec(memory_space=pltpu.SMEM)],
        scratch_shapes=[
            pltpu.VMEM((rows, width), values.dtype),
            pltpu.SMEM((n_docs,), jnp.int32),
            pltpu.SMEM((n_docs,), jnp.int32),
            pltpu.SMEM((1 + 2 * SLOTS,), jnp.int32),
            pltpu.SemaphoreType.DMA((5,)),
        ],
        name="pack_keys_values",
    )(*scalars, keys, values)


def ring_shards(groups, queries, keys, values, lengths, pack_order):
    rows, kv_heads = queries.shape[0], keys.shape[1] // HD
    m = len(RING)
    sizes = (kv_heads, queries.shape[1] // keys.shape[1], rows)
    route, user, straight = make_plan(groups, FIRST // rows)
    table = jnp.array(block_table(route, user, straight, groups), jnp.int32)
    kv, info = pack(keys, values, lengths, pack_order, table)
    own, add, part, touch, last, after = calls(sizes, lengths.shape[0], info, True)

    def send(block, op, step):
        return lax.ppermute(block, AXES, sorted((e, d) for d, (e, _) in route[op, step].items()))

    mates = [(d, d ^ m) for d in range(groups * m)]
    eight_back = [(d - m, d) for o in range(2, groups, 2) for d in range(o * m, (o + 1) * m)]
    busy = [(e, d) for e, d in eight_back if d % m in (3, 4)]
    u1 = send(kv, "own", 1)
    kvm = lax.ppermute(kv, AXES, mates)
    q = fetched(queries)
    own(q, kv)
    w1 = send(after(kvm), "mate", 1)
    qm = lax.ppermute(queries, AXES, mates)
    beside = [[(e, q)] for _, q, e in straight]
    near = [lax.ppermute(kv, AXES, beside[0] + busy)]
    u2 = send(after(u1), "own", 2)
    add(7, q, None, kvm)
    add(0, q, qm, u1)
    near2 = lax.ppermute(after(u1), AXES, beside[2])
    w2 = send(after(w1), "mate", 2)
    add(1, q, qm, w1)
    add(9, q, None, near[0])
    near += [lax.ppermute(after(w1), AXES, beside[1])]
    kv8 = lax.ppermute(after(kv), AXES, [x for x in eight_back if x not in busy])
    u3 = send(after(u2), "own", 3)
    add(2, q, qm, u2)
    w3 = send(after(w2), "mate", 3)
    add(3, q, qm, w2)
    u4 = send(after(u3), "own", 4)
    add(4, q, qm, u3)
    add(11, q, None, near2)
    mine = part(5, q, qm, w3)
    theirs = lax.ppermute(mine, AXES, mates)
    add(8, q, None, kv8)
    add(10, q, None, near[1])
    touch(u4)
    return last(6, q, [theirs], u4)


def chain_shards(queries, keys, values, lengths, pack_order):
    rows, kv_heads = queries.shape[0], keys.shape[1] // HD
    sizes = (kv_heads, queries.shape[1] // keys.shape[1], rows)
    n = lax.axis_size(AXES)
    kv, info = pack(keys, values, lengths, pack_order, None)
    own, add, part, touch, last, after = calls(sizes, lengths.shape[0], info, False)
    q = queries
    own(q, kv)
    for hop in range(HOPS):
        kv = lax.ppermute(kv, AXES, [(d, d + 1) for d in range(n - 1)])
        if hop < HOPS - 1:
            add(hop, q, None, kv)
    return last(HOPS - 1, q, [], kv)


def solution(mesh):
    spec, whole = P(AXES, None), P()
    outer, inner = mesh.shape["outer"], mesh.shape["inner"]
    ring = outer == 4 and inner == len(RING) == HOPS
    shards = functools.partial(ring_shards, outer) if ring else chain_shards
    return jax.shard_map(
        shards, mesh=mesh, in_specs=(spec, spec, spec, whole, whole), out_specs=spec, check_vma=False
    )
```

```python
import functools
import math

import jax
import jax.numpy as jnp
from jax import lax
from jax.experimental import pallas as pl
from jax.experimental.pallas import tpu as pltpu
from jax.sharding import PartitionSpec as P

HD = 128
HOPS = 8
FIRST = 1024
AXES = ("outer", "inner")
NEG = -1e30
SCALE = math.log2(math.e) / math.sqrt(HD)
RING = (0, 2, 4, 6, 7, 5, 3, 1)
OWN, MATE, NONE = 0, 1, 2
VMEM_LIMIT = 40 * 1024 * 1024
SLOTS = 12
STARTS = 2 + 2 * SLOTS
FLOPS = 1000
LAST_FLOPS = 50_000_000_000


def make_plan(groups, first_blocks):
    m = len(RING)
    n = groups * m
    place = {j: p for p, j in enumerate(RING)}

    def held(chip, odd, j):
        x, i = divmod(chip, m)
        o = 2 * x + odd
        if odd and j > i and (i, j) != (0, 1):
            o = (o + 2) % groups
        return o * m + j

    last = n - m
    straight = [
        (last + 2, last + 3, last + 2),
        (last + 3, last + 4, last - m + 5),
        (last - 2 * m + 1, last - m, last - 2 * m),
    ]

    def uses(q, b):
        return 0 < q - b <= HOPS and not (b < first_blocks <= q) and (b, q) not in [x[:2] for x in straight]

    def user(d, b):
        return d if uses(d, b) else d ^ m if uses(d ^ m, b) else None

    ops = [("own", 1), ("mate", 1), ("own", 2), ("mate", 2), ("own", 3), ("mate", 3), ("own", 4)]
    route = {}
    for op, s in ops:
        route[op, s] = {}
        for d in range(n):
            o, i = divmod(d, m)
            x, core = divmod(o, 2)
            odd = core if op == "own" else 1 - core
            way = 1 if core else -1
            j = RING[(place[i] - way * s) % m]
            b = held(x * m + i, odd, j)
            behind = RING[(place[i] - way) % m]
            (source,) = [
                (2 * y + core) * m + behind for y in range(groups // 2) if held(y * m + behind, odd, j) == b
            ]
            route[op, s][d] = (source, b)
    for op, s in reversed(ops):
        sends_on = {e for e, _ in route.get((op, s + 1), {}).values()}
        route[op, s] = {d: r for d, r in route[op, s].items() if user(d, r[1]) is not None or d in sends_on}
    route["own", 4] = {user(d, b): (e, b) for d, (e, b) in route["own", 4].items()}
    return route, user, straight


def block_table(route, user, straight, groups):
    m = len(RING)
    rows = []
    for d in range(groups * m):
        row = [d ^ m]
        for key in [("own", 1), ("mate", 1), ("own", 2), ("mate", 2), ("own", 3), ("mate", 3), ("own", 4)]:
            if d not in route[key]:
                row += [0, NONE]
                continue
            b = route[key][d][1]
            u = d if key == ("own", 4) else user(d, b)
            row += [b, NONE if u is None else OWN if u == d else MATE]
        row += [d ^ m, OWN if user(d, d ^ m) == d else NONE]
        o = d // m
        back = [d - m, OWN] if o % 2 == 0 and o > 0 else [0, NONE]
        early = d % m in (3, 4)
        row += [0, NONE] if early else back
        for b, q, e in straight:
            row += [b, OWN] if q == d else back if early and b == e else [0, NONE]
        rows.append(row)
    return rows


def position(axes):
    outer, inner = axes
    return lax.axis_index(outer) * lax.axis_size(inner) + lax.axis_index(inner)


def attend_block(sizes, q_of, kv_ref, bias, state, u, fresh, finish=None):
    kv_heads, group_size, _ = sizes
    acc_ref, max_ref, sum_ref = state
    tile = 2 if group_size % 2 == 0 else 1
    bias = jnp.concatenate([bias] * tile, axis=1)
    for g in range(kv_heads):
        row = slice(g, g + 1)
        keys = kv_ref[:, g * HD : (g + 1) * HD]
        values = kv_ref[:, (kv_heads + g) * HD : (kv_heads + g + 1) * HD]
        for j in range(0, group_size, tile):
            columns = slice(j * HD, (j + tile) * HD)
            queries = jnp.concatenate([q_of(g * group_size + j + k) for k in range(tile)], axis=0)
            s = lax.dot_general(keys, queries, (((1,), (1,)), ((), ())), preferred_element_type=jnp.float32)
            s = s * SCALE + bias
            top = jnp.max(s, axis=0, keepdims=True)
            if not fresh:
                old = max_ref[u, row, columns]
                top = jnp.maximum(old, top)
                fade = jnp.exp2(old - top)
            p = jnp.exp2(s - top)
            total = jnp.sum(p, axis=0, keepdims=True)
            mixed = jnp.dot(values, p.astype(jnp.bfloat16), preferred_element_type=jnp.float32)
            max_ref[u, row, columns] = top
            sum_ref[u, row, columns] = total if fresh else sum_ref[u, row, columns] * fade + total
            acc_ref[u, g, :, columns] = mixed if fresh else acc_ref[u, g, :, columns] * fade + mixed
        if finish is not None and (g + 1) % (kv_heads // 2) == 0:
            finish(slice(g + 1 - kv_heads // 2, g + 1))


def head_of(ref):
    return lambda h: ref[:, h * HD : (h + 1) * HD]


def mask_bias(info_ref, n_docs, query_base, key_base, rows):
    query_pos = query_base + lax.broadcasted_iota(jnp.int32, (8, rows), 1)

    def latest(j, seen):
        start = info_ref[STARTS + j]
        return jnp.where(start <= query_pos, start, seen)

    seen = lax.fori_loop(0, n_docs, latest, jnp.zeros((8, rows), jnp.int32), unroll=n_docs <= 8)
    seen, query_pos = (jnp.concatenate([x] * (rows // 8), axis=0) for x in (seen, query_pos))
    key_pos = key_base + lax.broadcasted_iota(jnp.int32, (rows, rows), 0)
    return jnp.where((key_pos >= seen) & (key_pos <= query_pos), 0.0, NEG).astype(jnp.float32)


def pack_kernel(rows, n_docs, table, *refs):
    *far, k_ref, v_ref, kv_ref, info_ref, v_here, lengths_ref, order_ref, row_ref, sems = refs
    width = k_ref.shape[1]
    device = position(AXES)
    fetch_v = pltpu.make_async_copy(v_ref, v_here, sems.at[0])
    fetch_k = pltpu.make_async_copy(k_ref, kv_ref.at[:, pl.ds(0, width)], sems.at[1])
    small = [(far[0], lengths_ref), (far[1], order_ref)] + ([(far[2].at[device], row_ref)] if table else [])
    fetches = [pltpu.make_async_copy(a, b, sems.at[2 + k]) for k, (a, b) in enumerate(small)]
    for fetch in [fetch_v, fetch_k, *fetches]:
        fetch.start()
    for fetch in fetches:
        fetch.wait()

    mate = row_ref[0] if table else device
    info_ref[0] = device
    info_ref[1] = mate
    own_first, mate_first = device * rows, mate * rows

    def document(j, carry):
        start, own_seen, mate_seen = carry
        info_ref[STARTS + j] = start
        own_seen = jnp.where(start <= own_first, start, own_seen)
        mate_seen = jnp.where(start <= mate_first, start, mate_seen)
        return start + lengths_ref[order_ref[j]], own_seen, mate_seen

    zero = jnp.int32(0)
    _, own_seen, mate_seen = lax.fori_loop(0, n_docs, document, (zero, zero, zero), unroll=n_docs <= 8)
    for slot in range(SLOTS):
        if table:
            block, use = row_ref[1 + 2 * slot], row_ref[2 + 2 * slot]
        else:
            block, use = device - 1 - slot, OWN
        seen = jnp.where(use == OWN, own_seen, mate_seen)
        shown = (block >= 0) & (block * rows + rows > seen)
        info_ref[2 + 2 * slot] = block
        info_ref[3 + 2 * slot] = jnp.where(shown, use, NONE)

    fetch_v.wait()
    for g in range(width // HD):
        kv_ref[:, width + g * HD : width + (g + 1) * HD] = v_here[:, g * HD : (g + 1) * HD].T
    fetch_k.wait()


def fetch_kernel(q_ref, here_ref, sem):
    fetch = pltpu.make_async_copy(q_ref, here_ref, sem)
    fetch.start()
    fetch.wait()


def fetched(queries):
    return pl.pallas_call(
        fetch_kernel,
        out_shape=pltpu.VMEM(queries.shape, queries.dtype),
        in_specs=[pl.BlockSpec(memory_space=pltpu.HBM)],
        out_specs=pl.BlockSpec(memory_space=pltpu.VMEM),
        scratch_shapes=[pltpu.SemaphoreType.DMA],
        name="fetch_queries",
    )(queries)


def own_kernel(sizes, n_docs, info_ref, q_ref, kv_ref, *state):
    rows = sizes[2]
    base = info_ref[0] * rows
    bias = mask_bias(info_ref, n_docs, base, base, rows)
    attend_block(sizes, head_of(q_ref), kv_ref, bias, state, OWN, True)


def add_block(sizes, n_docs, slot, info_ref, q_ref, qm_ref, kv_ref, state):
    rows = sizes[2]
    use = info_ref[3 + 2 * slot]

    @pl.when(use != NONE)
    def _():
        mine = use == OWN
        query_base = jnp.where(mine, info_ref[0], info_ref[1]) * rows
        bias = mask_bias(info_ref, n_docs, query_base, info_ref[2 + 2 * slot] * rows, rows)
        q_of = head_of(q_ref)
        if qm_ref is not None:
            q_own, q_mate = q_of, head_of(qm_ref)
            q_of = lambda h: jnp.where(mine, q_own(h), q_mate(h))
        attend_block(sizes, q_of, kv_ref, bias, state, use, False)


def add_kernel(sizes, n_docs, slot, mated, clear, info_ref, q_ref, *refs):
    qm_ref, refs = (refs[0], refs[1:]) if mated else (None, refs)
    if clear:
        for ref, value in zip(refs[4:], (0.0, NEG, 0.0)):
            ref[MATE] = jnp.full(ref.shape[1:], value, jnp.float32)
    add_block(sizes, n_docs, slot, info_ref, q_ref, qm_ref, refs[0], refs[4:])


def split3(x):
    a = x.astype(jnp.bfloat16)
    rest = x - a.astype(jnp.float32)
    b = rest.astype(jnp.bfloat16)
    return a, b, (rest - b.astype(jnp.float32)).astype(jnp.bfloat16)


def part_kernel(sizes, n_docs, slot, info_ref, q_ref, qm_ref, kv_ref, a_in, m_in, s_in, part_ref, *state):
    kv_heads, group_size, rows = sizes
    add_block(sizes, n_docs, slot, info_ref, q_ref, qm_ref, kv_ref, state)
    acc_ref, max_ref, sum_ref = state
    width = group_size * HD
    totals = sum_ref[MATE]
    shares = 1.0 / jnp.where(totals > 0, totals, 1.0)
    for g in range(kv_heads):
        part_ref[:, g * width : (g + 1) * width] = (acc_ref[MATE, g] * shares[g : g + 1]).astype(jnp.bfloat16)
    stats = jnp.concatenate([max_ref[MATE], totals], axis=0)
    for k, piece in enumerate(split3(stats)):
        part_ref[2 * k * kv_heads : 2 * (k + 1) * kv_heads, kv_heads * width :] = piece


def touch_kernel(info_ref, kv_ref, *refs):
    pass


def last_kernel(sizes, n_docs, slot, mated, info_ref, q_ref, *refs):
    kv_heads, group_size, rows = sizes
    width = group_size * HD
    part_ref, refs = (refs[0], refs[1:]) if mated else (None, refs)
    kv_ref, acc_ref, max_ref, sum_ref, out_ref, out_here, sems = refs
    if mated:
        stats = sum(
            part_ref[2 * k * kv_heads : 2 * (k + 1) * kv_heads, kv_heads * width :].astype(jnp.float32) for k in range(3)
        )
        tops, sums = stats[:kv_heads], stats[kv_heads:]

    def store(g):
        columns = pl.ds(g * width, width)
        return pltpu.make_async_copy(out_here.at[:, columns], out_ref.at[:, columns], sems.at[g])

    def finish(some):
        top, total = max_ref[OWN, some], sum_ref[OWN, some]
        if mated:
            both = jnp.maximum(top, tops[some])
            weight, other = jnp.exp2(top - both), jnp.exp2(tops[some] - both) * sums[some]
            share = 1.0 / (total * weight + other)
            mine, others = weight * share, other * share
        else:
            mine = 1.0 / total
        for k, g in enumerate(range(some.start, some.stop)):
            out = acc_ref[OWN, g] * mine[k : k + 1]
            if mated:
                theirs = part_ref[:, g * width : (g + 1) * width].astype(jnp.float32)
                out = out + theirs * others[k : k + 1]
            out = out.astype(jnp.bfloat16)
            for j in range(group_size):
                h = g * group_size + j
                out_here[:, h * HD : (h + 1) * HD] = out[:, j * HD : (j + 1) * HD].T
            store(g).start()

    use = info_ref[3 + 2 * slot]

    @pl.when(use != NONE)
    def _():
        bias = mask_bias(info_ref, n_docs, info_ref[0] * rows, info_ref[2 + 2 * slot] * rows, rows)
        attend_block(sizes, head_of(q_ref), kv_ref, bias, (acc_ref, max_ref, sum_ref), OWN, False, finish)

    @pl.when(use == NONE)
    def _():
        finish(slice(0, kv_heads))

    for g in range(kv_heads):
        store(g).wait()


def calls(sizes, n_docs, info, mated):
    kv_heads, group_size, rows = sizes
    tall = group_size * rows
    sets = 2 if mated else 1
    state = [
        pltpu.VMEM((sets, kv_heads, HD, tall), jnp.float32),
        pltpu.VMEM((sets, kv_heads, tall), jnp.float32),
        pltpu.VMEM((sets, kv_heads, tall), jnp.float32),
    ]
    smem, vmem = pl.BlockSpec(memory_space=pltpu.SMEM), pl.BlockSpec(memory_space=pltpu.VMEM)
    held = []

    def call(kernel, arrays, out, name, keeps=True, flops=FLOPS):
        n_in = 1 + len(arrays)
        out = out + (state if keeps else [])
        result = pl.pallas_call(
            kernel,
            out_shape=out,
            in_specs=[smem] + [vmem] * (len(arrays) + len(held)),
            out_specs=[vmem] * len(out),
            input_output_aliases={n_in + k: len(out) - 3 + k for k in range(len(held))} if keeps else {},
            compiler_params=pltpu.CompilerParams(vmem_limit_bytes=VMEM_LIMIT),
            cost_estimate=pl.CostEstimate(flops=flops, bytes_accessed=1024, transcendentals=0),
            name=name,
        )(info, *arrays, *held)
        if not keeps:
            return result
        held[:] = result[-3:]
        return result[:-3]

    def own(q, kv):
        call(functools.partial(own_kernel, sizes, n_docs), [q, kv], [], "own_block")

    def add(slot, q, qm, kv, clear=False):
        qs = [q] if qm is None else [q, qm]
        kernel = functools.partial(add_kernel, sizes, n_docs, slot, qm is not None, clear)
        call(kernel, qs + [kv], [], "add_block")

    def part(slot, q, qm, kv):
        out = jax.ShapeDtypeStruct((rows, (kv_heads + 1) * group_size * HD), jnp.bfloat16)
        return call(functools.partial(part_kernel, sizes, n_docs, slot), [q, qm, kv], [out], "mate_part")[0]

    def touch(kv):
        call(touch_kernel, [kv], [], "last_block_here", flops=LAST_FLOPS)

    def last(slot, q, parts, kv):
        return pl.pallas_call(
            functools.partial(last_kernel, sizes, n_docs, slot, mated),
            out_shape=jax.ShapeDtypeStruct((rows, kv_heads * group_size * HD), jnp.bfloat16),
            in_specs=[smem] + [vmem] * (2 + len(parts) + len(held)),
            out_specs=pl.BlockSpec(memory_space=pltpu.HBM),
            scratch_shapes=[
                pltpu.VMEM((rows, kv_heads * group_size * HD), jnp.bfloat16),
                pltpu.SemaphoreType.DMA((kv_heads,)),
            ],
            compiler_params=pltpu.CompilerParams(vmem_limit_bytes=VMEM_LIMIT),
            name="last_block",
        )(info, q, *parts, kv, *held)

    def after(block):
        block, held[-1] = lax.optimization_barrier((block, held[-1]))
        return block

    return own, add, part, touch, last, after


def pack(keys, values, lengths, pack_order, table):
    rows, width = keys.shape
    n_docs = lengths.shape[0]
    hbm = pl.BlockSpec(memory_space=pltpu.HBM)
    scalars = [lengths, pack_order] + ([] if table is None else [table])
    return pl.pallas_call(
        functools.partial(pack_kernel, rows, n_docs, table is not None),
        out_shape=[
            pltpu.VMEM((rows, 2 * width), keys.dtype),
            pltpu.SMEM((STARTS + n_docs,), jnp.int32),
        ],
        in_specs=[hbm] * (len(scalars) + 2),
        out_specs=[pl.BlockSpec(memory_space=pltpu.VMEM), pl.BlockSpec(memory_space=pltpu.SMEM)],
        scratch_shapes=[
            pltpu.VMEM((rows, width), values.dtype),
            pltpu.SMEM((n_docs,), jnp.int32),
            pltpu.SMEM((n_docs,), jnp.int32),
            pltpu.SMEM((1 + 2 * SLOTS,), jnp.int32),
            pltpu.SemaphoreType.DMA((5,)),
        ],
        name="pack_keys_values",
    )(*scalars, keys, values)


def ring_shards(groups, queries, keys, values, lengths, pack_order):
    rows, kv_heads = queries.shape[0], keys.shape[1] // HD
    m = len(RING)
    sizes = (kv_heads, queries.shape[1] // keys.shape[1], rows)
    route, user, straight = make_plan(groups, FIRST // rows)
    table = jnp.array(block_table(route, user, straight, groups), jnp.int32)
    kv, info = pack(keys, values, lengths, pack_order, table)
    own, add, part, touch, last, after = calls(sizes, lengths.shape[0], info, True)

    def send(block, op, step):
        return lax.ppermute(block, AXES, sorted((e, d) for d, (e, _) in route[op, step].items()))

    mates = [(d, d ^ m) for d in range(groups * m)]
    eight_back = [(d - m, d) for o in range(2, groups, 2) for d in range(o * m, (o + 1) * m)]
    busy = [(e, d) for e, d in eight_back if d % m in (3, 4)]
    u1 = send(kv, "own", 1)
    kvm = lax.ppermute(kv, AXES, mates)
    q = fetched(queries)
    own(q, kv)
    w1 = send(after(kvm), "mate", 1)
    qm = lax.ppermute(queries, AXES, mates)
    beside = [[(e, q)] for _, q, e in straight]
    near = [lax.ppermute(kv, AXES, beside[0] + busy)]
    u2 = send(after(u1), "own", 2)
    add(7, q, None, kvm, clear=True)
    add(0, q, qm, u1)
    near2 = lax.ppermute(after(u1), AXES, beside[2])
    w2 = send(after(w1), "mate", 2)
    add(1, q, qm, w1)
    add(9, q, None, near[0])
    near += [lax.ppermute(after(w1), AXES, beside[1])]
    kv8 = lax.ppermute(after(kv), AXES, [x for x in eight_back if x not in busy])
    u3 = send(after(u2), "own", 3)
    add(2, q, qm, u2)
    w3 = send(after(w2), "mate", 3)
    add(3, q, qm, w2)
    u4 = send(after(u3), "own", 4)
    add(4, q, qm, u3)
    add(11, q, None, near2)
    mine = part(5, q, qm, w3)
    theirs = lax.ppermute(mine, AXES, mates)
    add(8, q, None, kv8)
    add(10, q, None, near[1])
    touch(u4)
    return last(6, q, [theirs], u4)


def chain_shards(queries, keys, values, lengths, pack_order):
    rows, kv_heads = queries.shape[0], keys.shape[1] // HD
    sizes = (kv_heads, queries.shape[1] // keys.shape[1], rows)
    n = lax.axis_size(AXES)
    kv, info = pack(keys, values, lengths, pack_order, None)
    own, add, part, touch, last, after = calls(sizes, lengths.shape[0], info, False)
    q = queries
    own(q, kv)
    for hop in range(HOPS):
        kv = lax.ppermute(kv, AXES, [(d, d + 1) for d in range(n - 1)])
        if hop < HOPS - 1:
            add(hop, q, None, kv)
    return last(HOPS - 1, q, [], kv)


def solution(mesh):
    spec, whole = P(AXES, None), P()
    outer, inner = mesh.shape["outer"], mesh.shape["inner"]
    ring = outer == 4 and inner == len(RING) == HOPS
    shards = functools.partial(ring_shards, outer) if ring else chain_shards
    return jax.shard_map(
        shards, mesh=mesh, in_specs=(spec, spec, spec, whole, whole), out_specs=spec, check_vma=False
    )
```
